32 devices in a mesh: section: 2 (over x), tok: 4 (over y, core), head: 4 (over z).
Axes of the slice: x: 2, y: 2, z: 4, core: 2. Of those that a mesh axis runs over, the one named last changes fastest.
Arguments:
- block_input: bfloat16 [3, 2048, 768], P(None, ('tok', 'head')), may hold values from -6 to 6
- segment_ids: int32 [3, 2048], P(None, 'tok'), may hold values from 0 to 4, as said below
- output_grad: bfloat16 [3, 2048, 768], P(None, ('tok', 'head')), may hold values from -6 to 6
- norm_gains: bfloat16 [2, 2, 768], P('section'), may hold values from 0.5 to 1.5
- norm_biases: bfloat16 [2, 2, 768], P('section'), may hold values from -1 to 1
- qkv_weight: bfloat16 [2, 768, 3, 768], P('section', 'tok', None, 'head'), may hold values from -0.21875 to 0.21875
- qkv_bias: bfloat16 [2, 3, 768], P('section'), may hold values from -0.099609375 to 0.099609375
- feature_maps: bfloat16 [2, 12, 8192], P('section', 'head', 'tok'), may hold values from -2 to 2
- out_weight: bfloat16 [2, 768, 768], P('section', 'head', 'tok'), may hold values from -3 to 3
- branch_bias: bfloat16 [2, 2, 768], P('section'), may hold values from -0.59765625 to 0.59765625
- fc_weight: bfloat16 [2, 768, 3072], P('section', 'tok', 'head'), may hold values from -0.21875 to 0.21875
- fc_bias: bfloat16 [2, 3072], P('section'), may hold values from -0.59765625 to 0.59765625
- proj_weight: bfloat16 [2, 3072, 768], P('section', 'head', 'tok'), may hold values from -0.109375 to 0.109375
Outputs:
- layer_outputs: float32 [2, 3, 2048, 768], P('section', None, ('tok', 'head'))
- input_grads: float32 [2, 3, 2048, 768], P('section', None, ('tok', 'head'))
- norm_gain_grad: float32 [2, 2, 768], P('section')
- norm_bias_grad: float32 [2, 2, 768], P('section')
- qkv_weight_grad: float32 [2, 768, 3, 768], P('section', 'tok', None, 'head')
- qkv_bias_grad: float32 [2, 3, 768], P('section')
- feature_map_grad: float32 [2, 12, 8192], P('section', 'head', 'tok')
- out_weight_grad: float32 [2, 768, 768], P('section', 'head', 'tok')
- branch_bias_grad: float32 [2, 2, 768], P('section')
- fc_weight_grad: float32 [2, 768, 3072], P('section', 'tok', 'head')
- fc_bias_grad: float32 [2, 3072], P('section')
- proj_weight_grad: float32 [2, 3072, 768], P('section', 'head', 'tok')
The draws below stay inside these ranges and needn't reach their ends.
Inputs may be any that keep to these rules, and one draw needn't show every extreme that they name: `segment_ids`: each row is non-decreasing and holds five documents; document 2 starts among the first 512 tokens of the row and ends among its last 512.
All inputs are finite; a program needn't handle non-finite values.
Results may differ from the reference program's by a relative error of at most 0.04.
Values may be sent and summed in bfloat16 or wider, within the bound.
A program may use at most 192 MiB of HBM per device.

```python
import jax
import jax.numpy as jnp
from jax import lax

D = 768
H = 12
HS = 64
FF = 3072
FEATS = 128
SPAN = 64
TOK_DEV = 512
MICRO = 3
TOKENS = 2048
LAYERS = 2


def draw_segment_ids(key, part):
    key = jax.random.fold_in(key, 7)
    half = TOK_DEV // 2
    keys = jax.random.split(key, 4)
    first = jax.random.randint(keys[0], (MICRO, 1), 1, half)
    second = first + jax.random.randint(keys[1], (MICRO, 1), 1, half)
    fourth = TOKENS - jax.random.randint(keys[2], (MICRO, 1), 1, half)
    third = fourth - jax.random.randint(keys[3], (MICRO, 1), 1, half)
    place = jnp.arange(TOKENS, dtype=jnp.int32)[None, :]
    total = (place >= first).astype(jnp.int32) + (place >= second).astype(jnp.int32)
    total = total + (place >= third).astype(jnp.int32) + (place >= fourth).astype(jnp.int32)
    return total


def block_scale(stream_key, shape, cuts, low, top_value):
    level, own = 1.0, jax.random.fold_in(stream_key, 6)
    for dim, blocks in cuts:
        heights = jnp.exp(jax.random.uniform(jax.random.fold_in(own, dim), (blocks,), jnp.float32, low / len(cuts), top_value / len(cuts)))
        level = level * jnp.repeat(heights, shape[dim] // blocks).reshape([-1 if axis == dim else 1 for axis in range(len(shape))])
    return level


def normal_values(key, shape, deviation, limit, cuts=(), held_as=jnp.bfloat16):
    loudness = block_scale(key, shape, cuts, -0.22, 0.18) if cuts else 1.0
    values = jax.random.normal(key, shape, jnp.float32) * deviation * loudness
    return jnp.minimum(jnp.maximum(values, -limit), limit).astype(held_as)


def setup_inputs(seed: int = 0) -> dict:
    streams_of = jax.random.split(jax.random.key(seed), 14)
    return {
        "block_input": normal_values(streams_of[0], (MICRO, TOKENS, D), 1.0, 6.0, ((1, 16),)),
        "segment_ids": draw_segment_ids(jax.random.fold_in(streams_of[13], 71), 0),
        "output_grad": normal_values(streams_of[2], (MICRO, TOKENS, D), 1.0, 6.0, ((1, 16),)),
        "norm_gains": jnp.clip(1.0 + 0.1 * jax.random.normal(streams_of[3], (LAYERS, 2, D), jnp.float32), 0.5, 1.5).astype(jnp.bfloat16),
        "norm_biases": normal_values(streams_of[4], (LAYERS, 2, D), 0.2, 1.0, ((0, 2),)),
        "qkv_weight": normal_values(streams_of[5], (LAYERS, D, 3, D), D ** -0.5, 0.21875, ((0, 2), (1, 4), (3, 4))),
        "qkv_bias": normal_values(streams_of[6], (LAYERS, 3, D), 0.02, 0.099609375, ((0, 2),)),
        "feature_maps": normal_values(streams_of[7], (LAYERS, H, 2 * HS * HS), (HS // 8) ** -0.5, 2.0, ((0, 2), (1, 4), (2, 4))),
        "out_weight": normal_values(streams_of[8], (LAYERS, D, D), 4 ** -0.5, 3.0, ((0, 2), (1, 4), (2, 4))),
        "branch_bias": normal_values(streams_of[9], (LAYERS, 2, D), 0.1, 0.59765625, ((0, 2),)),
        "fc_weight": normal_values(streams_of[10], (LAYERS, D, FF), D ** -0.5, 0.21875, ((0, 2), (1, 4), (2, 4))),
        "fc_bias": normal_values(streams_of[11], (LAYERS, FF), 0.1, 0.59765625, ((0, 2),)),
        "proj_weight": normal_values(streams_of[12], (LAYERS, FF, D), FF ** -0.5, 0.109375, ((0, 2), (1, 4), (2, 4))),
    }


EPS = 1e-05
highest = lax.Precision.HIGHEST

@jax.custom_vjp
def low(v):
    return lax.optimization_barrier(v.astype(jnp.bfloat16)).astype(jnp.float32)

@jax.custom_vjp
def low_back(v):
    return v

def low_keep(v):
    return (low(v), None)

def low_pass(kept, grad):
    return (grad,)

def back_keep(v):
    return (v, None)

def back_low(kept, grad):
    return (low(grad),)
low.defvjp(low_keep, low_pass)
low_back.defvjp(back_keep, back_low)

def layer_norm(rows, gain, bias):
    center = lax.optimization_barrier(jnp.mean(rows, -1, keepdims=True))
    centred = rows - center
    spread = lax.optimization_barrier(jnp.mean(centred * centred, -1, keepdims=True))
    return centred * lax.rsqrt(spread + EPS) * gain + bias

def feature_map(logit):
    return jnp.concatenate([jax.nn.softmax(logit, -1), jax.nn.softmax(-logit, -1)], -1)

def attend(query_map, key_map, value_rows, segments):
    count = TOKENS // SPAN

    def to_blocks(rows):
        return rows.reshape(count, SPAN, H, rows.shape[-1]).transpose(0, 2, 1, 3)
    lower = jnp.arange(SPAN)[:, None] >= jnp.arange(SPAN)[None, :]
    ones_column = jnp.ones((H, SPAN, 1), jnp.float32)

    def block(carry, inputs):
        state, last = carry
        query, keyset, value, seg = inputs
        raw = jnp.einsum('htf,hsf->hts', query, keyset, precision=highest)
        mask = lower & (seg[:, None] == seg[None, :])
        scores = low(low_back(jnp.where(mask[None], raw, 0.0)))
        augmented = jnp.concatenate([value, ones_column], -1)
        inner = low_back(jnp.einsum('hts,hse->hte', scores, augmented, precision=highest))
        usable = (seg == last).astype(jnp.float32)[None, :, None]
        outer = jnp.einsum('htf,hef->hte', query, state, precision=highest) * usable
        total = inner + outer
        result = total[..., :HS] / total[..., HS:]
        kept = (seg == seg[-1]).astype(jnp.float32)[None, :, None]
        gained = jnp.einsum('hse,hsf->hef', augmented * kept, keyset, precision=highest)
        carried = (seg[-1] == last).astype(jnp.float32)
        return ((gained + carried * state, seg[-1]), result)
    start = (jnp.zeros((H, HS + 1, FEATS), jnp.float32), jnp.int32(-1))
    inputs = (to_blocks(query_map), to_blocks(key_map), to_blocks(value_rows), segments.reshape(count, SPAN))
    _, results = lax.scan(jax.checkpoint(block), start, inputs)
    return results.transpose(0, 2, 1, 3).reshape(TOKENS, H * HS)

def layer(params, residual, segments):
    gains, biases, weight_in, bias_in, maps, weight_out, branch, weight_up, bias_up, weight_down = params
    normed = low(layer_norm(residual, gains[0], biases[0]))
    projected = jnp.dot(normed, weight_in.reshape(D, 3 * D), precision=highest) + bias_in.reshape(3 * D)
    projected = low(low_back(projected)).reshape(TOKENS, 3, H, HS)
    mats = maps.reshape(H, 2, HS, HS)
    logits_q = low_back(jnp.einsum('the,hef->thf', projected[:, 0], mats[:, 0], precision=highest))
    logits_k = low_back(jnp.einsum('the,hef->thf', projected[:, 1], mats[:, 1], precision=highest))
    query_map = low(feature_map(logits_q))
    key_map = low(feature_map(logits_k))
    mixed = low(attend(query_map, key_map, projected[:, 2], segments))
    hidden = residual + (low_back(jnp.dot(mixed, weight_out, precision=highest)) + branch[0])
    middle = low(layer_norm(hidden, gains[1], biases[1]))
    before = low_back(jnp.dot(middle, weight_up, precision=highest) + bias_up)
    after = low(jax.nn.gelu(before, approximate=True))
    return hidden + (low_back(jnp.dot(after, weight_down, precision=highest)) + branch[1])

def reference(block_input, segment_ids, output_grad, norm_gains, norm_biases, qkv_weight, qkv_bias, feature_maps, out_weight, branch_bias, fc_weight, fc_bias, proj_weight):
    weights = [w.astype(jnp.float32) for w in (norm_gains, norm_biases, qkv_weight, qkv_bias, feature_maps, out_weight, branch_bias, fc_weight, fc_bias, proj_weight)]

    def run(params, inputs):
        return lax.map(lambda pair: layer(params, pair[0], pair[1]), (inputs, segment_ids))
    first_params = tuple((w[0] for w in weights))
    second_params = tuple((w[1] for w in weights))
    first, back_first = jax.vjp(run, first_params, block_input.astype(jnp.float32))
    second, back_second = jax.vjp(run, second_params, first)
    grads_second, grad_first = back_second(output_grad.astype(jnp.float32))
    grads_first, grad_input = back_first(grad_first)
    grads = [jnp.stack([early, late]) for early, late in zip(grads_first, grads_second)]
    return (jnp.stack([first, second]), jnp.stack([grad_input, grad_first]), grads[0], grads[1], grads[2], grads[3], grads[4], grads[5], grads[6], grads[7], grads[8], grads[9])
```

```python
import functools
import typing

import jax
import jax.numpy as jnp
from jax import lax
from jax.experimental import pallas as pl
from jax.experimental.pallas import tpu as pltpu
from jax.sharding import PartitionSpec as P

MESH = pl.DeviceIdType.MESH
EPS = 1e-05
F32 = jnp.float32
BF16 = jnp.bfloat16
NA = 4
CHUNK = 128
TILE = 768
UNROLL = 2


def dot_mid(left, right):
    return lax.dot_general(left, right, (((1,), (0,)), ((), ())), preferred_element_type=F32)


def dot_last(left, right):
    return lax.dot_general(left, right, (((1,), (1,)), ((), ())), preferred_element_type=F32)


def dot_first(left, right):
    return lax.dot_general(left, right, (((0,), (0,)), ((), ())), preferred_element_type=F32)


def norm_parts(rows):
    center = jnp.mean(rows, -1, keepdims=True)
    centred = rows - center
    spread = jnp.mean(centred * centred, -1, keepdims=True)
    scale = lax.rsqrt(spread + EPS)
    return centred * scale, scale


def norm_back(grad, gain, unit, scale):
    inner = grad * gain
    first = jnp.mean(inner, -1, keepdims=True)
    second = jnp.mean(inner * unit, -1, keepdims=True)
    return scale * (inner - first - unit * second)


def lanes(shape):
    return lax.broadcasted_iota(jnp.int32, shape, len(shape) - 1)


def column_sum(value):
    return jnp.sum(value, 0, keepdims=True)


class Sizes(typing.NamedTuple):
    tok: int
    head: int
    micro: int
    dmodel: int
    heads: int
    size: int
    ff: int
    ff_part: int
    shard: int
    state: int


class Step:
    def __init__(self, sizes, names, refs):
        self.sizes = sizes
        for name, ref in zip(names, refs):
            setattr(self, name, ref)

    def place(self):
        s = self.sizes
        self.section = lax.axis_index("section")
        self.tok = lax.axis_index("tok")
        self.z = lax.axis_index("head")
        group = s.tok // NA
        self.a = self.tok // group
        self.b = self.tok % group
        self.group = group
        self.y = self.a // 2
        self.c = self.a % 2
        self.n = s.tok * s.head
        self.home = self.tok * s.head + self.z
        r, core = self.tok // 2, self.tok % 2
        k = jnp.where(r % 2 == 0, self.z, s.head - 1 - self.z)
        self.p = r * (2 * s.head) + 2 * k + core

    def device_of_place(self, p):
        nz = self.sizes.head
        r = p // (2 * nz)
        k = (p % (2 * nz)) // 2
        z = jnp.where(r % 2 == 0, k, nz - 1 - k)
        return 2 * r + p % 2, z

    def cell(self, a, z):
        return {"tok": a * self.group + self.b, "head": z}

    def remote(self, src, dst, send, recv, device):
        return pltpu.make_async_remote_copy(
            src_ref=src, dst_ref=dst, send_sem=send, recv_sem=recv, device_id=device, device_id_type=MESH
        )

    def barrier(self):
        nt, nz = self.sizes.tok, self.sizes.head
        sem = pltpu.get_barrier_semaphore()

        def greet(k, carry):
            other = lax.rem(self.home + k, nt * nz)
            pl.semaphore_signal(
                sem,
                inc=1,
                device_id={"tok": other // nz, "head": other % nz},
                device_id_type=MESH,
            )
            return carry

        lax.fori_loop(1, nt * nz, greet, 0)
        pl.semaphore_signal(sem, inc=1, device_id={"section": 1 - self.section}, device_id_type=MESH)
        pl.semaphore_wait(sem, nt * nz)

    def take_params(self):
        for wide, ref in (
            (self.gains, self.gains_in),
            (self.biases, self.biases_in),
            (self.branch, self.branch_in),
            (self.bias_in, self.bias_in_in),
            (self.bias_up, self.bias_up_in),
        ):
            wide[...] = ref[...].astype(F32)
        here = pl.ds(pl.multiple_of(self.z * CHUNK, CHUNK), CHUNK)
        ahead = pl.ds(pl.multiple_of(jnp.maximum(self.z - 1, 0) * CHUNK, CHUNK), CHUNK)
        row = lax.broadcasted_iota(jnp.int32, (8, CHUNK), 0)
        for m in range(self.sizes.micro):
            ids = self.seg_ids[m : m + 1, here].astype(F32)
            before = self.seg_ids[m : m + 1, ahead].astype(F32)[:, CHUNK - 1 :]
            before = jnp.where(self.z > 0, before, jnp.where(self.tok > 0, 2.0, -1.0))
            self.seg_in[m] = jnp.where(row == 0, ids, jnp.where(row == 1, before, ids[:, CHUNK - 1 :]))

    def deal(self):
        for m in range(self.sizes.micro):
            q = self.n * m + self.home
            p, slot = q // 3, q % 3
            tok, z = self.device_of_place(p)
            here = p == self.p
            device = {"tok": tok, "head": z}

            @pl.when(here)
            def _():
                pltpu.make_async_copy(self.seg_in.at[m], self.segs.at[slot], self.segs_recv.at[slot]).start()

            @pl.when(jnp.logical_not(here))
            def _():
                self.remote(
                    self.seg_in.at[m], self.segs.at[slot], self.segs_send.at[m], self.segs_recv.at[slot], device
                ).start()

            for section, rows in enumerate((self.x_in, self.g_in)):
                mine = self.section == section

                @pl.when(mine & here)
                def _():
                    pltpu.make_async_copy(rows.at[m], self.land.at[0, slot], self.deal_recv.at[slot]).start()

                @pl.when(mine & jnp.logical_not(here))
                def _():
                    self.remote(
                        rows.at[m], self.land.at[0, slot], self.deal_send.at[m], self.deal_recv.at[slot], device
                    ).start()

    def dealt(self):
        for slot in range(3):
            q = 3 * self.p + slot
            here = q % self.n == self.home

            @pl.when(here)
            def _():
                pltpu.make_async_copy(self.x_in.at[0], self.land.at[0, slot], self.deal_recv.at[slot]).wait()
                pltpu.make_async_copy(self.seg_in.at[0], self.segs.at[slot], self.segs_recv.at[slot]).wait()

            @pl.when(jnp.logical_not(here))
            def _():
                device = {"tok": self.tok, "head": self.z}
                self.remote(
                    self.seg_in.at[0], self.segs.at[slot], self.segs_send.at[0], self.segs_recv.at[slot], device
                ).wait_recv()
                self.remote(
                    self.x_in.at[0], self.land.at[0, slot], self.deal_send.at[0], self.deal_recv.at[slot], device
                ).wait_recv()

    def deal_end(self):
        for m in range(self.sizes.micro):
            q = self.n * m + self.home

            @pl.when(q // 3 != self.p)
            def _():
                device = {"tok": self.tok, "head": self.z}
                self.remote(
                    self.seg_in.at[m], self.segs.at[0], self.segs_send.at[m], self.segs_recv.at[0], device
                ).wait_send()
                self.remote(
                    self.x_in.at[m], self.land.at[0, 0], self.deal_send.at[m], self.deal_recv.at[0], device
                ).wait_send()

    def send_home(self, index):
        out = (self.out_rows, self.grad_rows)[index]
        nz = self.sizes.head
        for slot in range(3):
            q = 3 * self.p + slot
            m, home = q // self.n, q % self.n
            here = home == self.home
            rows = self.cross.at[index, slot]
            recv = self.home_recv.at[index, m]

            @pl.when(here)
            def _():
                pltpu.make_async_copy(rows, out.at[m], recv).start()

            @pl.when(jnp.logical_not(here))
            def _():
                self.remote(
                    rows, out.at[m], self.home_send.at[index, slot], recv, {"tok": home // nz, "head": home % nz}
                ).start()

    def home_end(self, index):
        out = (self.out_rows, self.grad_rows)[index]
        device = {"tok": self.tok, "head": self.z}
        for slot in range(3):

            @pl.when((3 * self.p + slot) % self.n != self.home)
            def _():
                self.remote(
                    self.cross.at[index, slot],
                    out.at[0],
                    self.home_send.at[index, slot],
                    self.home_recv.at[index, 0],
                    device,
                ).wait_send()

        for m in range(self.sizes.micro):
            here = (self.n * m + self.home) // 3 == self.p
            recv = self.home_recv.at[index, m]

            @pl.when(here)
            def _():
                pltpu.make_async_copy(self.cross.at[index, 0], out.at[m], recv).wait()

            @pl.when(jnp.logical_not(here))
            def _():
                self.remote(
                    self.cross.at[index, 0], out.at[m], self.home_send.at[index, 0], recv, device
                ).wait_recv()

    def region(self, kind, a, z):
        s = self.sizes
        if kind == 0:
            return self.slab.at[a * s.head + z]
        full = self.fc if kind == 1 else self.pt
        rows, cols = s.shard, s.ff_part
        return full.at[pl.ds(pl.multiple_of(a * rows, 16), rows), pl.ds(pl.multiple_of(z * cols, 128), cols)]

    def towards(self, way):
        if way == 0:
            return self.cell(self.a, self.z + 1)
        if way == 1:
            return self.cell(self.a, self.z - 1)
        if way == 2:
            return self.cell(2 * (1 - self.y) + self.c, self.z)
        return self.cell(2 * self.y + 1 - self.c, self.z)

    def weight_copy(self, kind, a, z, way, own):
        s = self.sizes
        origin = a * s.head + z
        source = (self.sh_a, self.sh_f, self.sh_p)[kind] if own else self.region(kind, a, z)
        return self.remote(
            source,
            self.region(kind, a, z),
            self.ag_send.at[kind, way, origin],
            self.ag_recv.at[kind, origin],
            self.towards(way),
        )

    def weight_sends(self, kind, a, z, ways, own, act):
        for way in ways:
            if way == 0:
                pl.when(self.z < self.sizes.head - 1)(lambda: act(self.weight_copy(kind, a, z, 0, own)))
            elif way == 1:
                pl.when(self.z > 0)(lambda: act(self.weight_copy(kind, a, z, 1, own)))
            else:
                act(self.weight_copy(kind, a, z, way, own))

    def weight_own(self, kind):
        source = (self.sh_a, self.sh_f, self.sh_p)[kind]
        self.weight_sends(kind, self.a, self.z, (2, 0, 1, 3), True, lambda copy: copy.start())
        pltpu.make_async_copy(source, self.region(kind, self.a, self.z), self.ag_own.at[kind]).start()

    def weight_line(self, kind, d, act=None):
        start = act is None
        for sign, way in ((-1, 0), (1, 1)):
            z = self.z + sign * d
            inside = z >= 0 if sign < 0 else z < self.sizes.head

            @pl.when(inside)
            def _():
                if start:
                    self.weight_copy(kind, self.a, z, 2, False).wait_recv()
                self.weight_sends(
                    kind, self.a, z, (2, way, 3), False, (lambda copy: copy.start()) if start else act
                )

    def weight_cross(self, kind, d, act=None):
        start = act is None
        a = 2 * (1 - self.y) + self.c
        for sign in (-1, 1) if d else (1,):
            z = self.z + sign * d
            inside = (z >= 0) & (z < self.sizes.head)

            @pl.when(inside)
            def _():
                copy = self.weight_copy(kind, a, z, 3, False)
                if start:
                    copy.wait_recv()
                    copy.start()
                else:
                    act(copy)

    def weight_last(self, kind):
        for y in range(2):
            for z in range(self.sizes.head):
                self.weight_copy(kind, 2 * y + 1 - self.c, z, 3, False).wait_recv()
        source = (self.sh_a, self.sh_f, self.sh_p)[kind]
        pltpu.make_async_copy(source, self.region(kind, self.a, self.z), self.ag_own.at[kind]).wait()

    def weight_steps(self):
        nz = self.sizes.head
        steps = []
        for kind in range(3):
            for d in range(1, nz):
                steps.append(functools.partial(self.weight_line, kind, d))
                if d == 1 and kind < 2:
                    steps.append(functools.partial(self.weight_own, kind + 1))
            for d in range(nz):
                steps.append(functools.partial(self.weight_cross, kind, d))
            steps.append(functools.partial(self.weight_last, kind))
        return steps

    def weight_end(self, kind):
        nz = self.sizes.head
        finish = lambda copy: copy.wait_send()
        self.weight_sends(kind, self.a, self.z, (2, 0, 1, 3), True, finish)
        for d in range(1, nz):
            self.weight_line(kind, d, finish)
        for d in range(nz):
            self.weight_cross(kind, d, finish)

    def assemble(self):
        s = self.sizes
        nz, rows, heads = s.head, s.shard, s.heads // s.head
        width = heads * s.size
        dmodel = s.dmodel
        half = lanes((16, 128)) < 64
        for a in range(NA):
            for part in range(3):
                self.wq[a * rows : (a + 1) * rows, part * dmodel : (part + 1) * dmodel] = jnp.concatenate(
                    [self.slab[a * nz + z, 0:rows, part * width : (part + 1) * width] for z in range(nz)], 1
                )
        for z in range(nz):
            self.wo[z * width : (z + 1) * width, :] = jnp.concatenate(
                [self.slab[a * nz + z, 0:rows, 3 * width : 3 * width + rows] for a in range(NA)], 1
            )
        pairs = s.heads // 2
        for a in range(NA):
            for z in range(nz):
                for k in range(2 * heads):
                    head = heads * z + k // 2
                    block = self.slab[a * nz + z, rows : rows + 16, 128 * k : 128 * k + 128]
                    keep = half if head % 2 == 0 else jnp.logical_not(half)
                    first = 64 * (head % 2) + 32 * (a % 2) + 16 * (k % 2)
                    self.maps[(a // 2) * pairs + head // 2, first : first + 16, :] = jnp.where(
                        keep, block, jnp.zeros_like(block)
                    )

    def masks(self):
        for c in range(3):
            tile = self.segs[c]
            row = jnp.broadcast_to(tile[0:1], (CHUNK, CHUNK))
            column = row.T
            order = lax.broadcasted_iota(jnp.int32, (CHUNK, CHUNK), 0) >= lanes((CHUNK, CHUNK))
            self.causal[c] = jnp.where(order & (row == column), 1.0, 0.0)
            self.usable[c] = jnp.where(column == tile[1:2], 1.0, 0.0)
            self.kept[c] = jnp.where(column == tile[2:3], 1.0, 0.0)

    def linked(self, c):
        tile = self.segs[c]
        return jnp.where(tile[1:2] == tile[2:3], 1.0, 0.0)

    def head_sum(self, value):
        high = value.astype(BF16)
        low = (value - high.astype(F32)).astype(BF16)
        return dot_mid(jnp.concatenate([high, low], 1), self.ones[...])

    def norm_forward(self, rows, index, transposed, c):
        unit, _ = norm_parts(rows)
        low = (unit * self.gains[index : index + 1, :] + self.biases[index : index + 1, :]).astype(BF16)
        self.normed[c * CHUNK : (c + 1) * CHUNK, :] = low
        transposed[:, c * CHUNK : (c + 1) * CHUNK] = low.T

    def x_rows(self, c):
        return self.land[self.section, c].astype(F32)

    def project(self):
        s = self.sizes
        for c in range(3):
            self.norm_forward(self.x_rows(c), 0, self.normed_t, c)

        def tile(j, carry):
            cols = pl.ds(pl.multiple_of(j * TILE, TILE), TILE)
            value = dot_mid(self.normed[...], self.wq[:, cols]) + self.bias_in[pl.ds(j, 1), :]
            self.proj[:, cols] = value.astype(BF16)
            return carry

        lax.fori_loop(0, 3 * s.dmodel // TILE, tile, 0)

    def features(self, logits):
        left = lanes(logits.shape) < 64
        infinity = jnp.float32(jnp.inf)
        top = jnp.where(
            left,
            jnp.max(jnp.where(left, logits, -infinity), -1, keepdims=True),
            jnp.max(jnp.where(left, -infinity, logits), -1, keepdims=True),
        )
        bottom = jnp.where(
            left,
            jnp.min(jnp.where(left, logits, infinity), -1, keepdims=True),
            jnp.min(jnp.where(left, infinity, logits), -1, keepdims=True),
        )
        up = jnp.exp(logits - top)
        down = jnp.exp(bottom - logits)
        both = jnp.concatenate([up, down], 0)
        both = both / dot_mid(both.astype(BF16), self.ones[0:128, :])
        count = logits.shape[0]
        return jnp.concatenate([both[0:count], both[count:]], 1).astype(BF16)

    def columns(self, j, part):
        return pl.ds(pl.multiple_of(part * self.sizes.dmodel + j * 128, 128), 128)

    def compact(self, full):
        left = lanes((64, 128)) < 64
        return jnp.concatenate(
            [jnp.where(left, full[0:64], full[64:128]), jnp.where(left, full[128:192], full[192:256])], 0
        )

    def store_state(self, c, j, full):
        nrow = self.sizes.state - 128
        self.state[c, pl.ds(pl.multiple_of(j * 128, 128), 128), :] = self.compact(full[:, 0:128])
        norms = self.compact(full[:, 128:256])
        pick = lanes((128, 128)) % 64 == j
        self.state[c, nrow : nrow + 128, :] = jnp.where(pick, norms, self.state[c, nrow : nrow + 128, :])

    def expand(self, held, c, j):
        nrow = self.sizes.state - 128
        left = lanes((64, 128)) < 64
        zero = jnp.zeros((64, 128), F32)
        values = held[c, pl.ds(pl.multiple_of(j * 128, 128), 128), :].astype(F32)
        norms = held[c, nrow : nrow + 128, :].astype(F32)
        place = lanes((128, 128))
        norms = jnp.where(
            place < 64,
            jnp.sum(jnp.where(place == j, norms, 0.0), -1, keepdims=True),
            jnp.sum(jnp.where(place == 64 + j, norms, 0.0), -1, keepdims=True),
        )

        def spread(tile):
            up, down = tile[0:64], tile[64:128]
            return jnp.concatenate(
                [
                    jnp.where(left, up, zero),
                    jnp.where(left, zero, up),
                    jnp.where(left, down, zero),
                    jnp.where(left, zero, down),
                ],
                0,
            )

        return jnp.concatenate([spread(values), spread(norms)], 1).astype(BF16)

    def map_keys(self, step=None):
        pairs = self.sizes.heads // 2
        for c in range(3):
            self.state[c, self.sizes.state - 128 :, :] = jnp.zeros((128, 128), F32)

        def pair(j, carry):
            self.kmap[j] = self.features(dot_mid(self.proj[:, self.columns(j, 1)], self.maps[pairs + j]))
            for c in range(3):
                rows = slice(c * CHUNK, (c + 1) * CHUNK)
                kept = self.kept[c]
                held = (self.kmap[j, rows, :].astype(F32) * jnp.concatenate([kept, kept], 1)).astype(BF16)
                value = self.proj[rows, self.columns(j, 2)]
                full = dot_first(held, jnp.concatenate([value, jnp.ones_like(value)], 1))
                self.store_state(c, j, full)
            if step is not None:
                step(j)
            return carry

        lax.fori_loop(0, pairs, pair, 0, unroll=UNROLL)

    def map_queries(self):
        def pair(j, carry):
            self.qmap[j] = self.features(dot_mid(self.proj[:, self.columns(j, 0)], self.maps[j]))
            return carry

        lax.fori_loop(0, self.sizes.heads // 2, pair, 0, unroll=UNROLL)

    def chain_plan(self, forward):
        n = self.n
        enters = (3 * self.p) % n != 0
        leaves = (3 * (self.p + 1)) % n != 0
        if not forward:
            enters, leaves = leaves, enters
        cut = ((3 * self.p + 1) % n == 0) | ((3 * self.p + 2) % n == 0) | jnp.logical_not(enters)
        order = (0, 1, 2) if forward else (2, 1, 0)
        tok, z = self.device_of_place(jnp.clip(self.p + (1 if forward else -1), 0, n - 1))
        index = 0 if forward else 1
        message, landed, held = (
            (self.message, self.landed, self.enter)
            if forward
            else (self.message_back, self.landed_back, self.later)
        )
        copy = self.remote(
            message, landed, self.chain_send.at[index], self.chain_recv.at[index], {"tok": tok, "head": z}
        )
        return enters, leaves, cut, order, message, landed, held, copy

    def chain_sum(self, order):
        link = [self.linked(c) for c in order]
        return self.state[order[2]] + link[2] * (self.state[order[1]] + link[1] * self.state[order[0]])

    def chain_start(self, forward):
        enters, leaves, cut, order, message, landed, held, copy = self.chain_plan(forward)

        @pl.when(leaves & cut)
        def _():
            message[...] = self.chain_sum(order).astype(BF16)
            copy.start()

        @pl.when(leaves & jnp.logical_not(cut))
        def _():
            self.chain_own[...] = self.chain_sum(order)

    def chain_pass(self, forward):
        enters, leaves, cut, order, message, landed, held, copy = self.chain_plan(forward)

        @pl.when(enters)
        def _():
            copy.wait_recv()

        @pl.when(leaves & jnp.logical_not(cut))
        def _():
            passed = self.linked(0) * self.linked(1) * self.linked(2)
            message[...] = (self.chain_own[...] + passed * landed[...].astype(F32)).astype(BF16)
            copy.start()

        @pl.when(enters)
        def _():
            held[order[0]] = landed[...]

        @pl.when(jnp.logical_not(enters))
        def _():
            held[order[0]] = jnp.zeros_like(landed[...])

        for before, after in ((0, 1), (1, 2)):
            held[order[after]] = (
                self.state[order[before]] + self.linked(order[before]) * held[order[before]].astype(F32)
            ).astype(BF16)

    def chain_end(self, forward):
        enters, leaves, cut, order, message, landed, held, copy = self.chain_plan(forward)
        pl.when(leaves)(copy.wait_send)

    def attend_inner(self):
        pairs = self.sizes.heads // 2
        left = lanes((CHUNK, 128)) < 64
        ones = jnp.where(left, 1.0, 0.0).astype(BF16)
        others = jnp.where(left, 0.0, 1.0).astype(BF16)

        def pair(j, carry):
            for c in range(3):
                rows = slice(c * CHUNK, (c + 1) * CHUNK)
                query = self.qmap[j, rows, :]
                key = self.kmap[j, rows, :]
                value = self.proj[rows, self.columns(j, 2)]
                both = jnp.concatenate([ones, ones], 1), jnp.concatenate([others, others], 1)
                raw = dot_last(jnp.concatenate([query * both[0], query * both[1]], 0), key)
                mask = self.causal[c]
                scores = jnp.concatenate([raw[0:CHUNK] * mask, raw[CHUNK:] * mask], 1).astype(BF16)
                self.scores[j, rows, :] = scores
                spread = jnp.concatenate(
                    [
                        jnp.concatenate([value * ones, ones], 1),
                        jnp.concatenate([value * others, others], 1),
                    ],
                    0,
                )
                total = dot_mid(scores, spread)
                self.acc[rows, self.columns(j, 0)] = total[:, 0:128]
                self.denom[rows, self.columns(j, 0)] = total[:, 128:256]
            return carry

        lax.fori_loop(0, pairs, pair, 0, unroll=UNROLL)

    def attend_outer(self):
        def pair(j, carry):
            for c in range(3):
                rows = slice(c * CHUNK, (c + 1) * CHUNK)
                usable = self.usable[c]
                outer = dot_mid(self.qmap[j, rows, :], self.expand(self.enter, c, j))
                denom = self.denom[rows, self.columns(j, 0)] + usable * outer[:, 128:256]
                numer = self.acc[rows, self.columns(j, 0)] + usable * outer[:, 0:128]
                self.denom[rows, self.columns(j, 0)] = denom
                self.mixed[rows, self.columns(j, 0)] = (numer / denom).astype(BF16)
            return carry

        lax.fori_loop(0, self.sizes.heads // 2, pair, 0, unroll=UNROLL)

    def tiles(self, out, left, weight, act):
        width = 256

        def tile(j, carry):
            cols = pl.ds(pl.multiple_of(j * width, width), width)
            out[:, cols] = act(left, weight, cols)
            return carry

        lax.fori_loop(0, out.shape[1] // width, tile, 0, unroll=True)

    def attention_out(self):
        self.tiles(self.acc, self.mixed, self.wo, lambda l, w, cols: dot_mid(l[...], w[:, cols]))
        for c in range(3):
            rows = slice(c * CHUNK, (c + 1) * CHUNK)
            hidden = self.x_rows(c) + (self.acc[rows, :] + self.branch[0:1, :])
            self.hidden[rows, :] = hidden
            self.norm_forward(hidden, 1, self.middle_t, c)

    def feed_up(self):
        root = 0.7978845608028654

        def tile(j, carry):
            cols = pl.ds(pl.multiple_of(j * TILE, TILE), TILE)
            x = dot_mid(self.normed[...], self.fc[:, cols]) + self.bias_up[0:1, cols]
            square = x * x
            half = 0.5 * jnp.tanh(x * (root + (0.044715 * root) * square)) + 0.5
            self.after[:, cols] = (x * half).astype(BF16)
            inner = x * (2.0 * root + (6.0 * 0.044715 * root) * square)
            self.before[:, cols] = (half + (half - half * half) * inner).astype(BF16)
            return carry

        lax.fori_loop(0, self.sizes.ff // TILE, tile, 0)

    def feed_down(self):
        self.tiles(self.acc, self.after, self.pt, lambda l, w, cols: dot_last(l[...], w[cols, :]))
        for c in range(3):
            rows = slice(c * CHUNK, (c + 1) * CHUNK)
            out = self.hidden[rows, :] + (self.acc[rows, :] + self.branch[1:2, :])
            self.cross[0, c] = out.astype(BF16)
            pl.when(self.section == 0)(lambda: self.cross_copy(c).start())

    def cross_copy(self, c):
        return self.remote(
            self.cross.at[self.section, c],
            self.land.at[1, c],
            self.cross_send.at[c],
            self.cross_recv.at[c],
            {"section": 1 - self.section},
        )

    def g_rows(self, c):
        return self.land[1 - self.section, c]

    def take_grad(self):
        for c in range(3):
            rows = slice(c * CHUNK, (c + 1) * CHUNK)
            self.normed[rows, :] = self.g_rows(c)
            self.grad_t[:, rows] = self.g_rows(c).T

    def feed_back(self):
        def tile(j, carry):
            cols = pl.ds(pl.multiple_of(j * TILE, TILE), TILE)
            grad = dot_mid(self.normed[...], self.pt[:, cols])
            self.before[:, cols] = (grad * self.before[:, cols].astype(F32)).astype(BF16)
            return carry

        lax.fori_loop(0, self.sizes.ff // TILE, tile, 0)
        self.tiles(self.acc, self.before, self.fc, lambda l, w, cols: dot_last(l[...], w[cols, :]))
        sums = [0.0, 0.0, 0.0, 0.0]
        for c in range(3):
            rows = slice(c * CHUNK, (c + 1) * CHUNK)
            grad = self.acc[rows, :]
            g = self.g_rows(c).astype(F32)
            unit, scale = norm_parts(self.hidden[rows, :])
            through = g + norm_back(grad, self.gains[1:2, :], unit, scale)
            self.grad_hidden[rows, :] = through
            low = through.astype(BF16)
            self.normed[rows, :] = low
            for a in range(NA):
                width = self.sizes.shard
                self.low_parts[a, rows, :] = low[:, a * width : (a + 1) * width]
            for i, value in enumerate((grad * unit, grad, through, g)):
                sums[i] = sums[i] + column_sum(value)
        self.vec[1:2, :] = sums[0]
        self.vec[3:4, :] = sums[1]
        self.vec[4:5, :] = sums[2]
        self.vec[5:6, :] = sums[3]
        dmodel = self.sizes.dmodel
        for part in range(self.sizes.ff // dmodel):
            self.vec[9 + part : 10 + part, :] = column_sum(
                self.before[:, part * dmodel : (part + 1) * dmodel].astype(F32)
            )

    def mixed_back(self):
        self.tiles(self.acc, self.normed, self.wo, lambda l, w, cols: dot_last(l[...], w[cols, :]))

    def inner_grad(self, j):
        cols = self.columns(j, 0)
        inverse = 1.0 / self.denom[:, cols]
        grad = self.acc[:, cols] * inverse
        return grad, -self.head_sum(grad * self.mixed[:, cols].astype(F32))

    def state_back(self):
        for c in range(3):
            self.state[c, self.sizes.state - 128 :, :] = jnp.zeros((128, 128), F32)

        def pair(j, carry):
            numers, denoms = self.inner_grad(j)
            for c in range(3):
                rows = slice(c * CHUNK, (c + 1) * CHUNK)
                usable = self.usable[c]
                outer = jnp.concatenate([numers[rows] * usable, denoms[rows] * usable], 1).astype(BF16)
                self.store_state(c, j, dot_first(self.qmap[j, rows, :], outer))
            return carry

        lax.fori_loop(0, self.sizes.heads // 2, pair, 0, unroll=UNROLL)

    def softmax_back(self, kind, grad):
        count = kind.shape[0]
        grad = jnp.concatenate([grad[:, 0:128], grad[:, 128:256]], 0)
        kind = jnp.concatenate([kind[:, 0:128], kind[:, 128:256]], 0).astype(F32)
        part = kind * (grad - self.head_sum(kind * grad))
        return (part[0:count] - part[count:]).astype(BF16)

    def attend_back(self, step=None):
        pairs = self.sizes.heads // 2
        place = lanes((CHUNK, 128))
        left = place < 64
        ones = jnp.where(left, 1.0, 0.0).astype(BF16)
        others = jnp.where(left, 0.0, 1.0).astype(BF16)
        single = jnp.where(place == 0, 1.0, 0.0).astype(BF16)
        double = jnp.where(place == 64, 1.0, 0.0).astype(BF16)
        corner = jnp.where(place % 64 == 0, 1.0, 0.0).astype(BF16)

        def pair(j, carry):
            cols = self.columns(j, 0)
            numers, denoms = self.inner_grad(j)
            numers, denoms = numers.astype(BF16), denoms.astype(BF16)
            grads_query = []
            for c in range(3):
                rows = slice(c * CHUNK, (c + 1) * CHUNK)
                numer, denom = numers[rows], denoms[rows]
                value = self.proj[rows, self.columns(j, 2)]
                query = self.qmap[j, rows, :]
                key = self.kmap[j, rows, :]
                mask = self.causal[c]
                usable = self.usable[c]
                both = jnp.concatenate([ones, ones], 1), jnp.concatenate([others, others], 1)
                inner = jnp.concatenate(
                    [
                        jnp.concatenate([numer * ones, denom * single], 1),
                        jnp.concatenate([numer * others, denom * double], 1),
                    ],
                    0,
                )
                grads = dot_last(inner, jnp.concatenate([value, jnp.ones_like(value)], 1))
                early = (grads[0:CHUNK] * mask).astype(BF16)
                late = (grads[CHUNK:] * mask).astype(BF16)
                grad_query = dot_mid(
                    jnp.concatenate([early, late], 1),
                    jnp.concatenate([key * both[0], key * both[1]], 0),
                )
                state = self.expand(self.enter, c, j)
                grads_query.append(
                    grad_query
                    + jnp.concatenate([usable, usable], 1)
                    * dot_last(jnp.concatenate([numer, denom * corner], 1), state)
                )
                grad_key = dot_first(
                    jnp.concatenate([early, late], 0),
                    jnp.concatenate([query * both[0], query * both[1]], 0),
                )
                scores = self.scores[j, rows, :]
                grad_value = dot_first(
                    jnp.concatenate([scores[:, 0:CHUNK], scores[:, CHUNK:]], 0),
                    jnp.concatenate([numer * ones, numer * others], 0),
                )
                self.acc[rows, cols] = grad_value
                self.denom[rows, cols] = grad_key[:, 0:128]
                self.hidden[rows, cols] = grad_key[:, 128:256]
            logits = self.softmax_back(self.qmap[j], jnp.concatenate(grads_query, 0))
            self.grad_maps[j] = dot_first(self.proj[:, cols], logits)
            self.proj[:, cols] = dot_last(logits, self.maps[j]).astype(BF16)
            if step is not None:
                step(j)
            return carry

        lax.fori_loop(0, pairs, pair, 0, unroll=UNROLL)

    def attend_back_keys(self):
        pairs = self.sizes.heads // 2
        corner = jnp.where(lanes((CHUNK, 128)) % 64 == 0, 1.0, 0.0).astype(BF16)

        def pair(j, carry):
            cols = self.columns(j, 0)
            grads_key = []
            for c in range(3):
                rows = slice(c * CHUNK, (c + 1) * CHUNK)
                kept = self.kept[c]
                value = self.proj[rows, self.columns(j, 2)]
                later = self.expand(self.later, c, j)
                grad_key = jnp.concatenate([self.denom[rows, cols], self.hidden[rows, cols]], 1)
                grads_key.append(
                    grad_key
                    + jnp.concatenate([kept, kept], 1)
                    * dot_last(jnp.concatenate([value, corner], 1), later)
                )
                grad_value = self.acc[rows, cols] + kept * dot_mid(self.kmap[j, rows, :], later[:, 0:128])
                self.proj[rows, self.columns(j, 2)] = grad_value.astype(BF16)
            logits = self.softmax_back(self.kmap[j], jnp.concatenate(grads_key, 0))
            self.grad_maps[pairs + j] = dot_first(self.proj[:, self.columns(j, 1)], logits)
            self.proj[:, self.columns(j, 1)] = dot_last(logits, self.maps[pairs + j]).astype(BF16)
            return carry

        lax.fori_loop(0, pairs, pair, 0, unroll=UNROLL)

    def project_back(self):
        self.tiles(self.acc, self.proj, self.wq, lambda l, w, cols: dot_last(l[...], w[cols, :]))
        sums = [0.0, 0.0]
        for c in range(3):
            rows = slice(c * CHUNK, (c + 1) * CHUNK)
            grad = self.acc[rows, :]
            unit, scale = norm_parts(self.x_rows(c))
            total = self.grad_hidden[rows, :] + norm_back(grad, self.gains[0:1, :], unit, scale)
            self.cross[1, c] = total.astype(BF16)
            pl.when(self.section == 1)(lambda: self.cross_copy(c).start())
            sums[0] = sums[0] + column_sum(grad * unit)
            sums[1] = sums[1] + column_sum(grad)
        self.vec[0:1, :] = sums[0]
        self.vec[2:3, :] = sums[1]
        dmodel = self.sizes.dmodel
        for part in range(3):
            self.vec[6 + part : 7 + part, :] = column_sum(
                self.proj[:, part * dmodel : (part + 1) * dmodel].astype(F32)
            )

    def partial(self, kind, a, z):
        s = self.sizes
        rows = pl.ds(pl.multiple_of(a * s.shard, 16), s.shard)
        cols = slice(z * s.ff_part, (z + 1) * s.ff_part)
        if kind == 2:
            return dot_mid(self.grad_t[rows, :], self.after[:, cols])
        if kind == 1:
            return dot_mid(self.middle_t[rows, :], self.before[:, cols])
        heads = s.heads // s.head
        width = heads * s.size
        pairs = s.heads // 2
        left = self.normed_t[rows, :]
        pieces = [
            dot_mid(left, self.proj[:, part * s.dmodel + z * width : part * s.dmodel + (z + 1) * width])
            for part in range(3)
        ]
        pieces.append(dot_first(self.mixed[:, z * width : (z + 1) * width], self.low_parts[a]))
        top = jnp.concatenate(pieces, 1)
        half = lanes((16, 128)) < 64
        blocks = []
        for k in range(2 * heads):
            head = heads * z + k // 2
            first = pl.multiple_of(64 * (head % 2) + 32 * (a % 2) + 16 * (k % 2), 16)
            block = self.grad_maps[(a // 2) * pairs + head // 2, pl.ds(first, 16), :]
            keep = half if head % 2 == 0 else jnp.logical_not(half)
            block = jnp.where(keep, block, 0.0)
            blocks.append(block + pltpu.roll(block, 64, 1))
        return jnp.concatenate([top, jnp.concatenate(blocks, 1)], 0)

    def first_slot(self, kind, index):
        if kind == 0:
            return self.pair_a.at[index]
        return self.slab.at[8 * (kind - 1) + index, pl.ds(0, self.sizes.shard)]

    def slot_rows(self, ref, index, kind):
        rows = self.sizes.shard + (16 if kind == 0 else 0)
        return ref.at[kind, index, pl.ds(0, rows)]

    def pair_copy(self, kind, index):
        rows = self.sizes.shard + (16 if kind == 0 else 0)
        return self.remote(
            self.stage.at[index, pl.ds(0, rows)],
            self.first_slot(kind, index),
            self.pair_send.at[kind, index],
            self.pair_recv.at[kind, index],
            self.towards(3),
        )

    def reduce_pair(self, kind):
        nz = self.sizes.head
        rows = self.sizes.shard + (16 if kind == 0 else 0)
        for near in range(2):
            y = self.y if near else 1 - self.y
            for z in self.outward:
                index = near * nz + z
                if kind != self.kinds[0]:
                    self.pair_copy(self.kinds[self.kinds.index(kind) - 1], index).wait_send()
                self.stage[index, 0:rows, :] = self.partial(kind, 2 * y + 1 - self.c, z).astype(BF16)
                self.pair_copy(kind, index).start()

    def across_copy(self, kind, z):
        return self.remote(
            self.first_slot(kind, z),
            self.slot_rows(self.across, z, kind),
            self.across_send.at[kind, z],
            self.across_recv.at[kind, z],
            self.towards(2),
        )

    def reduce_across(self, kind):
        for z in self.outward:
            self.pair_copy(kind, z).wait_recv()
            slot = self.first_slot(kind, z)
            total = self.partial(kind, 2 * (1 - self.y) + self.c, z) + slot[...].astype(F32)
            slot[...] = total.astype(BF16)
            self.across_copy(kind, z).start()

    def reduce_here(self, kind, places):
        nz = self.sizes.head
        for z in places:
            self.pair_copy(kind, nz + z).wait_recv()
            total = self.partial(kind, 2 * self.y + self.c, z) + self.first_slot(kind, nz + z)[...].astype(F32)
            self.across_copy(kind, z).wait_recv()
            slot = self.slot_rows(self.across, z, kind)
            slot[...] = (total + slot[...].astype(F32)).astype(BF16)
            pl.when(self.z != z)(lambda: self.line_copy(kind, z).start())

    def line_copy(self, kind, z):
        nz = self.sizes.head
        index = (self.z - z + nz) % nz - 1
        return self.remote(
            self.slot_rows(self.across, z, kind),
            self.slot_rows(self.line, jnp.maximum(index, 0), kind),
            self.line_send.at[kind, z],
            self.line_recv.at[kind, jnp.maximum(index, 0)],
            self.cell(self.a, z),
        )

    def reduce_last(self, kind):
        nz = self.sizes.head
        source, out = self.reduced(kind)
        total = self.slot_rows(self.across, self.z, kind)[...].astype(F32)
        for index in range(nz - 1):
            slot = self.slot_rows(self.line, index, kind)
            self.remote(
                slot, slot, self.line_send.at[kind, 0], self.line_recv.at[kind, index], self.cell(self.a, self.z)
            ).wait_recv()
            total = total + slot[...].astype(F32)
        source[...] = total
        pltpu.make_async_copy(source, out, self.reduced_send.at[kind]).start()

    def reduced(self, kind):
        shard = self.sizes.shard
        if kind == 0:
            return self.denom.at[pl.ds(0, shard + 16)], self.grad_a
        if kind == 1:
            return self.acc.at[pl.ds(0, shard)], self.grad_f
        return self.acc.at[pl.ds(shard, shard)], self.grad_p

    def reduce_end(self):
        nz = self.sizes.head
        for kind in self.kinds:
            source, out = self.reduced(kind)
            pltpu.make_async_copy(source, out, self.reduced_send.at[kind]).wait()
        for z in range(2 * nz):
            self.pair_copy(self.kinds[-1], z).wait_send()
        for kind in self.kinds:
            for z in range(nz):
                self.across_copy(kind, z).wait_send()
            for z in range(nz):
                pl.when(self.z != z)(lambda: self.line_copy(kind, z).wait_send())

    def vector_copy(self, stage):
        nz = self.sizes.head
        device = (
            self.towards(3),
            self.towards(2),
            self.cell(self.a, self.z + 1 - 2 * (self.z % 2)),
            self.cell(self.a, (self.z + nz // 2) % nz),
        )[stage]
        return self.remote(
            self.vec_out.at[stage],
            self.vec_in.at[stage],
            self.vec_send.at[stage],
            self.vec_recv.at[stage],
            device,
        )

    def vector_start(self, stage):
        self.vec_out[stage] = self.vec[...]
        self.vector_copy(stage).start()

    def vector_end(self, stage):
        self.vector_copy(stage).wait_recv()
        self.vec[...] = self.vec[...] + self.vec_in[stage]

    def run(self):
        nz = self.sizes.head
        self.kinds = (2, 1, 0)
        self.outward = [z for pair in zip(range(nz // 2), range(nz - 1, nz // 2 - 1, -1)) for z in pair]
        self.place()
        first = self.section == 0
        second = self.section == 1
        self.take_params()
        self.barrier()
        self.weight_own(0)
        self.deal()
        place = lax.broadcasted_iota(jnp.int32, (256, 128), 0) % 128 // 64
        self.ones[...] = jnp.where(place == lanes((256, 128)) // 64, 1.0, 0.0).astype(BF16)
        self.vec[...] = jnp.zeros_like(self.vec)
        steps = self.weight_steps()
        count = len(steps) // 3 + 1
        for step in steps[:count]:
            step()
        steps = steps[count:]

        def all_weights():
            for step in steps:
                step()

        pl.when(second)(all_weights)
        at = [0]

        def some_weights(number):
            taken = steps[at[0] : at[0] + number]
            at[0] += number

            @pl.when(first)
            def _():
                for step in taken:
                    step()

        self.assemble()
        self.dealt()
        self.masks()
        some_weights(1)
        for c in range(3):
            pl.when(second)(lambda: self.cross_copy(c).wait_recv())
        self.project()
        some_weights(1)

        def between(j):
            for k in range(3):

                @pl.when(first & (j == 2 * k + 1))
                def _():
                    steps[at[0] + k]()

        self.map_keys(between)
        at[0] += 3
        self.chain_start(True)
        self.map_queries()
        self.attend_inner()
        self.chain_pass(True)
        some_weights(2)
        self.attend_outer()
        some_weights(1)
        self.attention_out()
        some_weights(2)
        self.feed_up()
        some_weights(len(steps))
        self.weight_end(0)
        pl.semaphore_signal(self.free, inc=1, device_id=self.towards(3), device_id_type=MESH)
        self.feed_down()

        @pl.when(first)
        def _():
            self.send_home(0)
            for c in range(3):
                self.cross_copy(c).wait_recv()

        self.take_grad()

        @pl.when(first)
        def _():
            pl.semaphore_wait(self.free, 1)
            self.reduce_pair(2)
            self.reduce_across(2)

        self.feed_back()

        hold = self.p % (2 * nz) < 2
        pl.when(first)(lambda: self.reduce_pair(1))
        self.mixed_back()
        self.state_back()
        self.chain_start(False)
        pl.when(first & jnp.logical_not(hold))(lambda: self.reduce_across(1))
        n = self.n
        depth = (((3 * self.p + 2) // n + 1) * n - 1) // 3 - self.p
        when = jnp.minimum(jnp.maximum(2 * depth - 2, 0), self.sizes.heads // 2 - 1)

        def during(j):
            pl.when(j == when)(lambda: self.chain_pass(False))

        self.attend_back(during)

        pl.when(first & hold)(lambda: self.reduce_across(1))
        pl.when(first)(lambda: self.reduce_here(2, self.outward))
        self.attend_back_keys()
        self.project_back()

        self.vector_start(0)

        @pl.when(second)
        def _():
            pl.semaphore_wait(self.free, 1)
            self.reduce_pair(2)
            self.reduce_across(2)
            self.reduce_pair(1)
            self.reduce_across(1)

        self.reduce_pair(0)
        self.vector_end(0)
        self.vector_start(1)
        self.reduce_across(0)
        pl.when(second)(lambda: self.send_home(0))
        self.send_home(1)
        pl.when(second)(lambda: self.reduce_here(2, self.outward))
        self.vector_end(1)
        self.vector_start(2)
        self.reduce_here(1, self.outward)
        self.vector_end(2)
        self.vector_start(3)
        self.reduce_last(2)
        self.reduce_here(0, self.outward)
        self.reduce_last(1)
        self.vector_end(3)
        self.reduce_last(0)
        for stage in range(4):
            self.vector_copy(stage).wait_send()
        self.grad_gains[...] = self.vec[0:2, :]
        self.grad_biases[...] = self.vec[2:4, :]
        self.grad_branch[...] = self.vec[4:6, :]
        self.grad_bias_in[...] = self.vec[6:9, :]
        dmodel = self.sizes.dmodel
        for part in range(self.sizes.ff // dmodel):
            self.grad_bias_up[:, part * dmodel : (part + 1) * dmodel] = self.vec[9 + part : 10 + part, :]
        self.deal_end()
        self.weight_end(1)
        self.weight_end(2)
        for c in range(3):
            self.cross_copy(c).wait_send()
        self.chain_end(True)
        self.chain_end(False)
        self.reduce_end()
        self.home_end(0)
        self.home_end(1)


def scratch(s):
    rows, dmodel, ff, shard = 3 * CHUNK, s.dmodel, s.ff, s.shard
    pairs, nz, state = s.heads // 2, s.head, s.state
    vmem, dma = pltpu.VMEM, pltpu.SemaphoreType.DMA
    cells = NA * nz
    return dict(
        seg_in=vmem((3, 8, CHUNK), F32),
        gains=vmem((2, dmodel), F32),
        biases=vmem((2, dmodel), F32),
        branch=vmem((2, dmodel), F32),
        bias_in=vmem((3, dmodel), F32),
        bias_up=vmem((1, ff), F32),
        vec=vmem((16, dmodel), F32),
        land=vmem((2, 3, CHUNK, dmodel), BF16),
        segs=vmem((3, 8, CHUNK), F32),
        slab=vmem((cells, shard + 16, dmodel), BF16),
        fc=vmem((dmodel, ff), BF16),
        pt=vmem((dmodel, ff), BF16),
        wq=vmem((dmodel, 3 * dmodel), BF16),
        wo=vmem((dmodel, dmodel), BF16),
        maps=vmem((2 * pairs, 128, 128), BF16),
        ones=vmem((256, 128), BF16),
        causal=vmem((3, CHUNK, CHUNK), F32),
        usable=vmem((3, CHUNK, CHUNK), F32),
        kept=vmem((3, CHUNK, CHUNK), F32),
        normed=vmem((rows, dmodel), BF16),
        normed_t=vmem((dmodel, rows), BF16),
        middle_t=vmem((dmodel, rows), BF16),
        grad_t=vmem((dmodel, rows), BF16),
        proj=vmem((rows, 3 * dmodel), BF16),
        qmap=vmem((pairs, rows, 256), BF16),
        kmap=vmem((pairs, rows, 256), BF16),
        scores=vmem((pairs, rows, 256), BF16),
        denom=vmem((rows, dmodel), F32),
        mixed=vmem((rows, dmodel), BF16),
        acc=vmem((rows, dmodel), F32),
        hidden=vmem((rows, dmodel), F32),
        grad_hidden=vmem((rows, dmodel), F32),
        after=vmem((rows, ff), BF16),
        before=vmem((rows, ff), BF16),
        low_parts=vmem((NA, rows, shard), BF16),
        cross=vmem((2, 3, CHUNK, dmodel), BF16),
        state=vmem((3, state, 128), F32),
        chain_own=vmem((state, 128), F32),
        enter=vmem((3, state, 128), BF16),
        later=vmem((3, state, 128), BF16),
        message=vmem((state, 128), BF16),
        landed=vmem((state, 128), BF16),
        message_back=vmem((state, 128), BF16),
        landed_back=vmem((state, 128), BF16),
        grad_maps=vmem((2 * pairs, 128, 128), F32),
        stage=vmem((2 * nz, shard + 16, dmodel), BF16),
        pair_a=vmem((2 * nz, shard + 16, dmodel), BF16),
        across=vmem((3, nz, shard + 16, dmodel), BF16),
        line=vmem((3, nz - 1, shard + 16, dmodel), BF16),
        vec_out=vmem((4, 16, dmodel), F32),
        vec_in=vmem((4, 16, dmodel), F32),
        deal_send=dma((3,)),
        deal_recv=dma((3,)),
        segs_send=dma((3,)),
        segs_recv=dma((3,)),
        ag_send=dma((3, 4, cells)),
        ag_recv=dma((3, cells)),
        ag_own=dma((3,)),
        cross_send=dma((3,)),
        cross_recv=dma((3,)),
        chain_send=dma((2,)),
        chain_recv=dma((2,)),
        home_send=dma((2, 3)),
        home_recv=dma((2, 3)),
        pair_send=dma((3, 2 * nz)),
        pair_recv=dma((3, 2 * nz)),
        across_send=dma((3, nz)),
        across_recv=dma((3, nz)),
        line_send=dma((3, nz)),
        line_recv=dma((3, nz - 1)),
        reduced_send=dma((3,)),
        vec_send=dma((4,)),
        vec_recv=dma((4,)),
        free=pltpu.SemaphoreType.REGULAR,
    )


def train_step(s, *args):
    held = scratch(s)
    anywhere = pl.BlockSpec(memory_space=pl.ANY)
    inside = pl.BlockSpec(memory_space=pltpu.VMEM)
    dmodel, shard = s.dmodel, s.shard
    given = dict(
        x_in=anywhere,
        g_in=anywhere,
        seg_ids=inside,
        sh_a=anywhere,
        sh_f=anywhere,
        sh_p=anywhere,
        gains_in=inside,
        biases_in=inside,
        branch_in=inside,
        bias_in_in=inside,
        bias_up_in=inside,
    )
    made = dict(
        out_rows=anywhere,
        grad_rows=anywhere,
        grad_a=anywhere,
        grad_f=anywhere,
        grad_p=anywhere,
        grad_gains=inside,
        grad_biases=inside,
        grad_branch=inside,
        grad_bias_in=inside,
        grad_bias_up=inside,
    )
    names = list(given) + list(made) + list(held)

    def body(*refs):
        Step(s, names, refs).run()

    return pl.pallas_call(
        body,
        out_shape=(
            jax.ShapeDtypeStruct((3, CHUNK, dmodel), BF16),
            jax.ShapeDtypeStruct((3, CHUNK, dmodel), BF16),
            jax.ShapeDtypeStruct((shard + 16, dmodel), F32),
            jax.ShapeDtypeStruct((shard, dmodel), F32),
            jax.ShapeDtypeStruct((shard, dmodel), F32),
            jax.ShapeDtypeStruct((2, dmodel), F32),
            jax.ShapeDtypeStruct((2, dmodel), F32),
            jax.ShapeDtypeStruct((2, dmodel), F32),
            jax.ShapeDtypeStruct((3, dmodel), F32),
            jax.ShapeDtypeStruct((1, s.ff), F32),
        ),
        in_specs=list(given.values()),
        out_specs=tuple(made.values()),
        scratch_shapes=list(held.values()),
        compiler_params=pltpu.CompilerParams(
            collective_id=0, has_side_effects=True, vmem_limit_bytes=64 * 1024 * 1024
        ),
        name="train_step",
    )(*args)


def local(
    block_input,
    segment_ids,
    output_grad,
    norm_gains,
    norm_biases,
    qkv_weight,
    qkv_bias,
    feature_maps,
    out_weight,
    branch_bias,
    fc_weight,
    fc_bias,
    proj_weight,
):
    nt, nz = lax.axis_size("tok"), lax.axis_size("head")
    micro, rows, dmodel = block_input.shape
    heads = feature_maps.shape[1] * nz
    ff = fc_bias.shape[1]
    size = dmodel // heads
    group = nt // NA
    sizes = Sizes(
        tok=nt,
        head=nz,
        micro=micro,
        dmodel=dmodel,
        heads=heads,
        size=size,
        ff=ff,
        ff_part=ff // nz,
        shard=dmodel // NA,
        state=heads // 2 * 128 + 128,
    )
    assert micro == 3 and rows == CHUNK and size == 64 and nt % NA == 0
    groups = [[group * a + b for b in range(group)] for a in range(NA)]

    def widen(part, dim):
        if group == 1:
            return part
        return lax.all_gather(part, "tok", axis=dim, tiled=True, axis_index_groups=groups)

    def narrow(part, dim):
        if group == 1:
            return part
        return lax.psum_scatter(part, "tok", scatter_dimension=dim, tiled=True, axis_index_groups=groups)

    shard = dmodel // NA
    width = dmodel // nz
    w_in = widen(qkv_weight[0], 0).reshape(shard, 3 * width)
    w_out = widen(out_weight[0], 1)
    maps = widen(feature_maps[0], 1)
    w_up = widen(fc_weight[0], 0)
    w_down = widen(proj_weight[0], 1).T
    maps = maps.reshape(2 * heads // nz, 16, size)
    maps = jnp.concatenate([maps, maps], 2).transpose(1, 0, 2).reshape(16, 4 * heads // nz * size)
    sh_a = jnp.concatenate([jnp.concatenate([w_in, w_out], 1), maps], 0)
    out_rows, grad_rows, grad_a, grad_f, grad_p, *vectors = train_step(
        sizes,
        block_input,
        output_grad,
        segment_ids,
        sh_a,
        w_up,
        w_down,
        norm_gains[0],
        norm_biases[0],
        branch_bias[0],
        qkv_bias[0],
        fc_bias,
    )
    if group > 1:
        vectors = [jnp.sum(lax.all_gather(v, "tok", axis=0, axis_index_groups=groups), 0) for v in vectors]
    grad_in = narrow(grad_a[:shard, : 3 * width].reshape(shard, 3, width), 0)
    grad_out = narrow(grad_a[:shard, 3 * width :], 1)
    grad_maps = grad_a[shard:].reshape(16, 2 * heads // nz, 2 * size)[:, :, :size]
    grad_maps = narrow(grad_maps.transpose(1, 0, 2).reshape(heads // nz, 2 * 16 * size), 1)
    return (
        out_rows[None].astype(F32),
        grad_rows[None].astype(F32),
        vectors[0][None],
        vectors[1][None],
        grad_in[None],
        vectors[3][None],
        grad_maps[None],
        grad_out[None],
        vectors[2][None],
        narrow(grad_f, 0)[None],
        vectors[4],
        narrow(grad_p, 0).T[None],
    )


def solution(mesh):
    in_specs = (
        P(None, ("tok", "head"), None),
        P(None, "tok"),
        P(None, ("tok", "head"), None),
        P("section", None, None),
        P("section", None, None),
        P("section", "tok", None, "head"),
        P("section", None, None),
        P("section", "head", "tok"),
        P("section", "head", "tok"),
        P("section", None, None),
        P("section", "tok", "head"),
        P("section", None),
        P("section", "head", "tok"),
    )
    out_specs = (
        P("section", None, ("tok", "head"), None),
        P("section", None, ("tok", "head"), None),
        P("section", None, None),
        P("section", None, None),
        P("section", "tok", None, "head"),
        P("section", None, None),
        P("section", "head", "tok"),
        P("section", "head", "tok"),
        P("section", None, None),
        P("section", "tok", "head"),
        P("section", None),
        P("section", "head", "tok"),
    )
    return jax.shard_map(local, mesh=mesh, in_specs=in_specs, out_specs=out_specs, check_vma=False)
```

```python
import functools
import typing

import jax
import jax.numpy as jnp
from jax import lax
from jax.experimental import pallas as pl
from jax.experimental.pallas import tpu as pltpu
from jax.sharding import PartitionSpec as P

MESH = pl.DeviceIdType.MESH
EPS = 1e-05
F32 = jnp.float32
BF16 = jnp.bfloat16
NA = 4
CHUNK = 128
TILE = 768
UNROLL = 2


def dot_mid(left, right):
    return lax.dot_general(left, right, (((1,), (0,)), ((), ())), preferred_element_type=F32)


def dot_last(left, right):
    return lax.dot_general(left, right, (((1,), (1,)), ((), ())), preferred_element_type=F32)


def dot_first(left, right):
    return lax.dot_general(left, right, (((0,), (0,)), ((), ())), preferred_element_type=F32)


def norm_parts(rows):
    center = jnp.mean(rows, -1, keepdims=True)
    centred = rows - center
    spread = jnp.mean(centred * centred, -1, keepdims=True)
    scale = lax.rsqrt(spread + EPS)
    return centred * scale, scale


def norm_back(grad, gain, unit, scale):
    inner = grad * gain
    first = jnp.mean(inner, -1, keepdims=True)
    second = jnp.mean(inner * unit, -1, keepdims=True)
    return scale * (inner - first - unit * second)


def lanes(shape):
    return lax.broadcasted_iota(jnp.int32, shape, len(shape) - 1)


def column_sum(value):
    return jnp.sum(value, 0, keepdims=True)


class Sizes(typing.NamedTuple):
    tok: int
    head: int
    micro: int
    dmodel: int
    heads: int
    size: int
    ff: int
    ff_part: int
    shard: int
    state: int


class Step:
    def __init__(self, sizes, names, refs):
        self.sizes = sizes
        for name, ref in zip(names, refs):
            setattr(self, name, ref)

    def place(self):
        s = self.sizes
        self.section = lax.axis_index("section")
        self.tok = lax.axis_index("tok")
        self.z = lax.axis_index("head")
        group = s.tok // NA
        self.a = self.tok // group
        self.b = self.tok % group
        self.group = group
        self.y = self.a // 2
        self.c = self.a % 2
        self.n = s.tok * s.head
        self.home = self.tok * s.head + self.z
        r, core = self.tok // 2, self.tok % 2
        k = jnp.where(r % 2 == 0, self.z, s.head - 1 - self.z)
        self.p = r * (2 * s.head) + 2 * k + core

    def device_of_place(self, p):
        nz = self.sizes.head
        r = p // (2 * nz)
        k = (p % (2 * nz)) // 2
        z = jnp.where(r % 2 == 0, k, nz - 1 - k)
        return 2 * r + p % 2, z

    def cell(self, a, z):
        return {"tok": a * self.group + self.b, "head": z}

    def remote(self, src, dst, send, recv, device):
        return pltpu.make_async_remote_copy(
            src_ref=src, dst_ref=dst, send_sem=send, recv_sem=recv, device_id=device, device_id_type=MESH
        )

    def barrier(self):
        nt, nz = self.sizes.tok, self.sizes.head
        sem = pltpu.get_barrier_semaphore()

        def greet(k, carry):
            other = lax.rem(self.home + k, nt * nz)
            pl.semaphore_signal(
                sem,
                inc=1,
                device_id={"tok": other // nz, "head": other % nz},
                device_id_type=MESH,
            )
            return carry

        lax.fori_loop(1, nt * nz, greet, 0)
        pl.semaphore_signal(sem, inc=1, device_id={"section": 1 - self.section}, device_id_type=MESH)
        pl.semaphore_signal(sem, inc=1, device_id=self.corner(), device_id_type=MESH)
        pl.semaphore_wait(sem, nt * nz + 1)

    def take_params(self):
        for wide, ref in (
            (self.gains, self.gains_in),
            (self.biases, self.biases_in),
            (self.branch, self.branch_in),
            (self.bias_in, self.bias_in_in),
            (self.bias_up, self.bias_up_in),
        ):
            wide[...] = ref[...].astype(F32)
        here = pl.ds(pl.multiple_of(self.z * CHUNK, CHUNK), CHUNK)
        ahead = pl.ds(pl.multiple_of(jnp.maximum(self.z - 1, 0) * CHUNK, CHUNK), CHUNK)
        row = lax.broadcasted_iota(jnp.int32, (8, CHUNK), 0)
        for m in range(self.sizes.micro):
            ids = self.seg_ids[m : m + 1, here].astype(F32)
            before = self.seg_ids[m : m + 1, ahead].astype(F32)[:, CHUNK - 1 :]
            before = jnp.where(self.z > 0, before, jnp.where(self.tok > 0, 2.0, -1.0))
            self.seg_in[m] = jnp.where(row == 0, ids, jnp.where(row == 1, before, ids[:, CHUNK - 1 :]))

    def deal(self):
        for m in range(self.sizes.micro):
            q = self.n * m + self.home
            p, slot = q // 3, q % 3
            tok, z = self.device_of_place(p)
            here = p == self.p
            device = {"tok": tok, "head": z}

            @pl.when(here)
            def _():
                pltpu.make_async_copy(self.seg_in.at[m], self.segs.at[slot], self.segs_recv.at[slot]).start()

            @pl.when(jnp.logical_not(here))
            def _():
                self.remote(
                    self.seg_in.at[m], self.segs.at[slot], self.segs_send.at[m], self.segs_recv.at[slot], device
                ).start()

            for section, rows in enumerate((self.x_in, self.g_in)):
                mine = self.section == section

                @pl.when(mine & here)
                def _():
                    pltpu.make_async_copy(rows.at[m], self.land.at[0, slot], self.deal_recv.at[slot]).start()

                @pl.when(mine & jnp.logical_not(here))
                def _():
                    self.remote(
                        rows.at[m], self.land.at[0, slot], self.deal_send.at[m], self.deal_recv.at[slot], device
                    ).start()

    def dealt(self):
        for slot in range(3):
            q = 3 * self.p + slot
            here = q % self.n == self.home

            @pl.when(here)
            def _():
                pltpu.make_async_copy(self.x_in.at[0], self.land.at[0, slot], self.deal_recv.at[slot]).wait()
                pltpu.make_async_copy(self.seg_in.at[0], self.segs.at[slot], self.segs_recv.at[slot]).wait()

            @pl.when(jnp.logical_not(here))
            def _():
                device = {"tok": self.tok, "head": self.z}
                self.remote(
                    self.seg_in.at[0], self.segs.at[slot], self.segs_send.at[0], self.segs_recv.at[slot], device
                ).wait_recv()
                self.remote(
                    self.x_in.at[0], self.land.at[0, slot], self.deal_send.at[0], self.deal_recv.at[slot], device
                ).wait_recv()

    def deal_end(self):
        for m in range(self.sizes.micro):
            q = self.n * m + self.home

            @pl.when(q // 3 != self.p)
            def _():
                device = {"tok": self.tok, "head": self.z}
                self.remote(
                    self.seg_in.at[m], self.segs.at[0], self.segs_send.at[m], self.segs_recv.at[0], device
                ).wait_send()
                self.remote(
                    self.x_in.at[m], self.land.at[0, 0], self.deal_send.at[m], self.deal_recv.at[0], device
                ).wait_send()

    def send_home(self, index):
        out = (self.out_rows, self.grad_rows)[index]
        nz = self.sizes.head
        for slot in range(3):
            q = 3 * self.p + slot
            m, home = q // self.n, q % self.n
            here = home == self.home
            rows = self.cross.at[index, slot]
            recv = self.home_recv.at[index, m]

            @pl.when(here)
            def _():
                pltpu.make_async_copy(rows, out.at[m], recv).start()

            @pl.when(jnp.logical_not(here))
            def _():
                self.remote(
                    rows, out.at[m], self.home_send.at[index, slot], recv, {"tok": home // nz, "head": home % nz}
                ).start()

    def home_end(self, index):
        out = (self.out_rows, self.grad_rows)[index]
        device = {"tok": self.tok, "head": self.z}
        for slot in range(3):

            @pl.when((3 * self.p + slot) % self.n != self.home)
            def _():
                self.remote(
                    self.cross.at[index, slot],
                    out.at[0],
                    self.home_send.at[index, slot],
                    self.home_recv.at[index, 0],
                    device,
                ).wait_send()

        for m in range(self.sizes.micro):
            here = (self.n * m + self.home) // 3 == self.p
            recv = self.home_recv.at[index, m]

            @pl.when(here)
            def _():
                pltpu.make_async_copy(self.cross.at[index, 0], out.at[m], recv).wait()

            @pl.when(jnp.logical_not(here))
            def _():
                self.remote(
                    self.cross.at[index, 0], out.at[m], self.home_send.at[index, 0], recv, device
                ).wait_recv()

    def region(self, kind, a, z):
        s = self.sizes
        if kind == 0:
            return self.slab.at[a * s.head + z]
        full = self.fc if kind == 1 else self.pt
        rows, cols = s.shard, s.ff_part
        return full.at[pl.ds(pl.multiple_of(a * rows, 16), rows), pl.ds(pl.multiple_of(z * cols, 128), cols)]

    def towards(self, way):
        if way == 0:
            return self.cell(self.a, self.z + 1)
        if way == 1:
            return self.cell(self.a, self.z - 1)
        if way == 2:
            return self.cell(2 * (1 - self.y) + self.c, self.z)
        return self.cell(2 * self.y + 1 - self.c, self.z)

    def weight_copy(self, kind, a, z, way, own):
        s = self.sizes
        origin = a * s.head + z
        source = (self.sh_a, self.sh_f, self.sh_p)[kind] if own else self.region(kind, a, z)
        return self.remote(
            source,
            self.region(kind, a, z),
            self.ag_send.at[kind, way, origin],
            self.ag_recv.at[kind, origin],
            self.towards(way),
        )

    def corner(self):
        return {"section": 1 - self.section, **self.towards(2)}

    def relay_slot(self, z):
        s = self.sizes
        return self.after.at[pl.ds(0, s.shard), pl.ds(pl.multiple_of(z * s.ff_part, 128), s.ff_part)]

    def relay_in(self, z, own):
        return self.remote(
            self.sh_p if own else self.region(2, self.a, z),
            self.relay_slot(z),
            self.ag_send.at[2, 2, self.a * self.sizes.head + z],
            self.relay_recv.at[z],
            self.corner(),
        )

    def relay_out(self, z):
        a = 2 * (1 - self.y) + self.c
        return self.remote(
            self.relay_slot(z),
            self.region(2, a, z),
            self.relay_send.at[z],
            self.ag_recv.at[2, a * self.sizes.head + z],
            {"section": 1 - self.section},
        )

    def relay(self, d, end=False):
        for sign in (-1, 1) if d else (1,):
            z = self.z + sign * d

            @pl.when((z >= 0) & (z < self.sizes.head))
            def _():
                if end:
                    self.relay_out(z).wait_send()
                else:
                    self.relay_in(z, False).wait_recv()
                    self.relay_out(z).start()

    def weight_sends(self, kind, a, z, ways, own, act):
        for way in ways:
            if kind == 2 and way == 2:
                pl.when(self.section == 0)(lambda: act(self.relay_in(z, own)))
                pl.when(self.section == 1)(lambda: act(self.weight_copy(kind, a, z, 2, own)))
            elif way == 0:
                pl.when(self.z < self.sizes.head - 1)(lambda: act(self.weight_copy(kind, a, z, 0, own)))
            elif way == 1:
                pl.when(self.z > 0)(lambda: act(self.weight_copy(kind, a, z, 1, own)))
            else:
                act(self.weight_copy(kind, a, z, way, own))

    def weight_own(self, kind):
        source = (self.sh_a, self.sh_f, self.sh_p)[kind]
        self.weight_sends(kind, self.a, self.z, (2, 0, 1, 3), True, lambda copy: copy.start())
        pltpu.make_async_copy(source, self.region(kind, self.a, self.z), self.ag_own.at[kind]).start()

    def weight_line(self, kind, d, act=None):
        start = act is None
        for sign, way in ((-1, 0), (1, 1)):
            z = self.z + sign * d
            inside = z >= 0 if sign < 0 else z < self.sizes.head

            @pl.when(inside)
            def _():
                if start:
                    self.weight_copy(kind, self.a, z, 3, False).wait_recv()
                self.weight_sends(
                    kind, self.a, z, (2, way, 3), False, (lambda copy: copy.start()) if start else act
                )

    def weight_cross(self, kind, d, act=None):
        start = act is None
        a = 2 * (1 - self.y) + self.c
        for sign in (-1, 1) if d else (1,):
            z = self.z + sign * d
            inside = (z >= 0) & (z < self.sizes.head)

            @pl.when(inside)
            def _():
                copy = self.weight_copy(kind, a, z, 3, False)
                if start:
                    copy.wait_recv()
                    copy.start()
                else:
                    act(copy)

    def weight_last(self, kind):
        for y in range(2):
            for z in range(self.sizes.head):
                self.weight_copy(kind, 2 * y + 1 - self.c, z, 3, False).wait_recv()
        source = (self.sh_a, self.sh_f, self.sh_p)[kind]
        pltpu.make_async_copy(source, self.region(kind, self.a, self.z), self.ag_own.at[kind]).wait()

    def weight_steps(self):
        nz = self.sizes.head
        line = lambda kind, d: functools.partial(self.weight_line, kind, d)
        cross = lambda kind, d: functools.partial(self.weight_cross, kind, d)
        own = lambda kind: functools.partial(self.weight_own, kind)
        last = lambda kind: functools.partial(self.weight_last, kind)
        relay = lambda d: functools.partial(self.relay, d)
        start = [line(0, 1), own(1)] + [line(0, d) for d in range(2, nz)]
        start += [cross(0, d) for d in range(nz)] + [last(0)]
        one = [line(1, 1), own(2)] + [line(1, d) for d in range(2, nz)] + [cross(1, 0)]
        for d in range(1, nz):
            one += [cross(1, d), line(2, d)]
        one += [last(1)] + [cross(2, d) for d in range(nz)] + [last(2)]
        two = [line(1, 1), own(2)] + [line(1, d) for d in range(2, nz)]
        for d in range(nz):
            two += [relay(d), cross(1, d)]
        two += [last(1)] + [line(2, d) for d in range(1, nz)]
        return start, one, two, [cross(2, d) for d in range(nz)] + [last(2)]

    def weight_end(self, kind):
        nz = self.sizes.head
        finish = lambda copy: copy.wait_send()
        self.weight_sends(kind, self.a, self.z, (2, 0, 1, 3), True, finish)
        for d in range(1, nz):
            self.weight_line(kind, d, finish)
        for d in range(nz):
            self.weight_cross(kind, d, finish)

    def assemble(self):
        s = self.sizes
        nz, rows, heads = s.head, s.shard, s.heads // s.head
        width = heads * s.size
        dmodel = s.dmodel
        half = lanes((16, 128)) < 64
        for a in range(NA):
            for part in range(3):
                self.wq[a * rows : (a + 1) * rows, part * dmodel : (part + 1) * dmodel] = jnp.concatenate(
                    [self.slab[a * nz + z, 0:rows, part * width : (part + 1) * width] for z in range(nz)], 1
                )
        for z in range(nz):
            self.wo[z * width : (z + 1) * width, :] = jnp.concatenate(
                [self.slab[a * nz + z, 0:rows, 3 * width : 3 * width + rows] for a in range(NA)], 1
            )
        pairs = s.heads // 2
        for a in range(NA):
            for z in range(nz):
                for k in range(2 * heads):
                    head = heads * z + k // 2
                    block = self.slab[a * nz + z, rows : rows + 16, 128 * k : 128 * k + 128]
                    keep = half if head % 2 == 0 else jnp.logical_not(half)
                    first = 64 * (head % 2) + 32 * (a % 2) + 16 * (k % 2)
                    self.maps[(a // 2) * pairs + head // 2, first : first + 16, :] = jnp.where(
                        keep, block, jnp.zeros_like(block)
                    )

    def masks(self):
        for c in range(3):
            tile = self.segs[c]
            row = jnp.broadcast_to(tile[0:1], (CHUNK, CHUNK))
            column = row.T
            order = lax.broadcasted_iota(jnp.int32, (CHUNK, CHUNK), 0) >= lanes((CHUNK, CHUNK))
            self.causal[c] = jnp.where(order & (row == column), 1.0, 0.0)
            self.usable[c] = jnp.where(column == tile[1:2], 1.0, 0.0)
            self.kept[c] = jnp.where(column == tile[2:3], 1.0, 0.0)

    def linked(self, c):
        tile = self.segs[c]
        return jnp.where(tile[1:2] == tile[2:3], 1.0, 0.0)

    def head_sum(self, value):
        high = value.astype(BF16)
        low = (value - high.astype(F32)).astype(BF16)
        return dot_mid(jnp.concatenate([high, low], 1), self.ones[...])

    def norm_forward(self, rows, index, transposed, c):
        unit, _ = norm_parts(rows)
        low = (unit * self.gains[index : index + 1, :] + self.biases[index : index + 1, :]).astype(BF16)
        self.normed[c * CHUNK : (c + 1) * CHUNK, :] = low
        transposed[:, c * CHUNK : (c + 1) * CHUNK] = low.T

    def x_rows(self, c):
        return self.land[self.section, c].astype(F32)

    def project(self):
        s = self.sizes
        for c in range(3):
            self.norm_forward(self.x_rows(c), 0, self.normed_t, c)

        def tile(j, carry):
            cols = pl.ds(pl.multiple_of(j * TILE, TILE), TILE)
            value = dot_mid(self.normed[...], self.wq[:, cols]) + self.bias_in[pl.ds(j, 1), :]
            self.proj[:, cols] = value.astype(BF16)
            return carry

        lax.fori_loop(0, 3 * s.dmodel // TILE, tile, 0)

    def features(self, logits):
        left = lanes(logits.shape) < 64
        infinity = jnp.float32(jnp.inf)
        top = jnp.where(
            left,
            jnp.max(jnp.where(left, logits, -infinity), -1, keepdims=True),
            jnp.max(jnp.where(left, -infinity, logits), -1, keepdims=True),
        )
        bottom = jnp.where(
            left,
            jnp.min(jnp.where(left, logits, infinity), -1, keepdims=True),
            jnp.min(jnp.where(left, infinity, logits), -1, keepdims=True),
        )
        up = jnp.exp(logits - top)
        down = jnp.exp(bottom - logits)
        both = jnp.concatenate([up, down], 0)
        both = both / dot_mid(both.astype(BF16), self.ones[0:128, :])
        count = logits.shape[0]
        return jnp.concatenate([both[0:count], both[count:]], 1).astype(BF16)

    def columns(self, j, part):
        return pl.ds(pl.multiple_of(part * self.sizes.dmodel + j * 128, 128), 128)

    def compact(self, full):
        left = lanes((64, 128)) < 64
        return jnp.concatenate(
            [jnp.where(left, full[0:64], full[64:128]), jnp.where(left, full[128:192], full[192:256])], 0
        )

    def store_state(self, c, j, full):
        nrow = self.sizes.state - 128
        self.state[c, pl.ds(pl.multiple_of(j * 128, 128), 128), :] = self.compact(full[:, 0:128])
        norms = self.compact(full[:, 128:256])
        pick = lanes((128, 128)) % 64 == j
        self.state[c, nrow : nrow + 128, :] = jnp.where(pick, norms, self.state[c, nrow : nrow + 128, :])

    def expand(self, held, c, j):
        nrow = self.sizes.state - 128
        left = lanes((64, 128)) < 64
        zero = jnp.zeros((64, 128), F32)
        values = held[c, pl.ds(pl.multiple_of(j * 128, 128), 128), :].astype(F32)
        norms = held[c, nrow : nrow + 128, :].astype(F32)
        place = lanes((128, 128))
        norms = jnp.where(
            place < 64,
            jnp.sum(jnp.where(place == j, norms, 0.0), -1, keepdims=True),
            jnp.sum(jnp.where(place == 64 + j, norms, 0.0), -1, keepdims=True),
        )

        def spread(tile):
            up, down = tile[0:64], tile[64:128]
            return jnp.concatenate(
                [
                    jnp.where(left, up, zero),
                    jnp.where(left, zero, up),
                    jnp.where(left, down, zero),
                    jnp.where(left, zero, down),
                ],
                0,
            )

        return jnp.concatenate([spread(values), spread(norms)], 1).astype(BF16)

    def map_keys(self, step=None):
        pairs = self.sizes.heads // 2
        for c in range(3):
            self.state[c, self.sizes.state - 128 :, :] = jnp.zeros((128, 128), F32)

        def pair(j, carry):
            self.kmap[j] = self.features(dot_mid(self.proj[:, self.columns(j, 1)], self.maps[pairs + j]))
            for c in range(3):
                rows = slice(c * CHUNK, (c + 1) * CHUNK)
                kept = self.kept[c]
                held = (self.kmap[j, rows, :].astype(F32) * jnp.concatenate([kept, kept], 1)).astype(BF16)
                value = self.proj[rows, self.columns(j, 2)]
                full = dot_first(held, jnp.concatenate([value, jnp.ones_like(value)], 1))
                self.store_state(c, j, full)
            if step is not None:
                step(j)
            return carry

        lax.fori_loop(0, pairs, pair, 0, unroll=UNROLL)

    def map_queries(self):
        def pair(j, carry):
            self.qmap[j] = self.features(dot_mid(self.proj[:, self.columns(j, 0)], self.maps[j]))
            return carry

        lax.fori_loop(0, self.sizes.heads // 2, pair, 0, unroll=UNROLL)

    def chain_plan(self, forward):
        n = self.n
        enters = (3 * self.p) % n != 0
        leaves = (3 * (self.p + 1)) % n != 0
        if not forward:
            enters, leaves = leaves, enters
        cut = ((3 * self.p + 1) % n == 0) | ((3 * self.p + 2) % n == 0) | jnp.logical_not(enters)
        order = (0, 1, 2) if forward else (2, 1, 0)
        tok, z = self.device_of_place(jnp.clip(self.p + (1 if forward else -1), 0, n - 1))
        index = 0 if forward else 1
        message, landed, held = (
            (self.message, self.landed, self.enter)
            if forward
            else (self.message_back, self.landed_back, self.later)
        )
        copy = self.remote(
            message, landed, self.chain_send.at[index], self.chain_recv.at[index], {"tok": tok, "head": z}
        )
        return enters, leaves, cut, order, message, landed, held, copy

    def chain_sum(self, order):
        link = [self.linked(c) for c in order]
        return self.state[order[2]] + link[2] * (self.state[order[1]] + link[1] * self.state[order[0]])

    def chain_start(self, forward):
        enters, leaves, cut, order, message, landed, held, copy = self.chain_plan(forward)

        @pl.when(leaves & cut)
        def _():
            message[...] = self.chain_sum(order).astype(BF16)
            copy.start()

        @pl.when(leaves & jnp.logical_not(cut))
        def _():
            self.chain_own[...] = self.chain_sum(order)

    def chain_pass(self, forward):
        enters, leaves, cut, order, message, landed, held, copy = self.chain_plan(forward)

        @pl.when(enters)
        def _():
            copy.wait_recv()

        @pl.when(leaves & jnp.logical_not(cut))
        def _():
            passed = self.linked(0) * self.linked(1) * self.linked(2)
            message[...] = (self.chain_own[...] + passed * landed[...].astype(F32)).astype(BF16)
            copy.start()

        @pl.when(enters)
        def _():
            held[order[0]] = landed[...]

        @pl.when(jnp.logical_not(enters))
        def _():
            held[order[0]] = jnp.zeros_like(landed[...])

        for before, after in ((0, 1), (1, 2)):
            held[order[after]] = (
                self.state[order[before]] + self.linked(order[before]) * held[order[before]].astype(F32)
            ).astype(BF16)

    def chain_end(self, forward):
        enters, leaves, cut, order, message, landed, held, copy = self.chain_plan(forward)
        pl.when(leaves)(copy.wait_send)

    def attend_inner(self, step=None):
        pairs = self.sizes.heads // 2
        left = lanes((CHUNK, 128)) < 64
        ones = jnp.where(left, 1.0, 0.0).astype(BF16)
        others = jnp.where(left, 0.0, 1.0).astype(BF16)

        def pair(j, carry):
            for c in range(3):
                rows = slice(c * CHUNK, (c + 1) * CHUNK)
                query = self.qmap[j, rows, :]
                key = self.kmap[j, rows, :]
                value = self.proj[rows, self.columns(j, 2)]
                both = jnp.concatenate([ones, ones], 1), jnp.concatenate([others, others], 1)
                raw = dot_last(jnp.concatenate([query * both[0], query * both[1]], 0), key)
                mask = self.causal[c]
                scores = jnp.concatenate([raw[0:CHUNK] * mask, raw[CHUNK:] * mask], 1).astype(BF16)
                self.scores[j, rows, :] = scores
                spread = jnp.concatenate(
                    [
                        jnp.concatenate([value * ones, ones], 1),
                        jnp.concatenate([value * others, others], 1),
                    ],
                    0,
                )
                total = dot_mid(scores, spread)
                self.acc[rows, self.columns(j, 0)] = total[:, 0:128]
                self.denom[rows, self.columns(j, 0)] = total[:, 128:256]
            if step is not None:
                step(j)
            return carry

        lax.fori_loop(0, pairs, pair, 0, unroll=UNROLL)

    def attend_outer(self):
        def pair(j, carry):
            for c in range(3):
                rows = slice(c * CHUNK, (c + 1) * CHUNK)
                usable = self.usable[c]
                outer = dot_mid(self.qmap[j, rows, :], self.expand(self.enter, c, j))
                denom = self.denom[rows, self.columns(j, 0)] + usable * outer[:, 128:256]
                numer = self.acc[rows, self.columns(j, 0)] + usable * outer[:, 0:128]
                self.denom[rows, self.columns(j, 0)] = denom
                self.mixed[rows, self.columns(j, 0)] = (numer / denom).astype(BF16)
            return carry

        lax.fori_loop(0, self.sizes.heads // 2, pair, 0, unroll=UNROLL)

    def tiles(self, out, left, weight, act):
        width = 256

        def tile(j, carry):
            cols = pl.ds(pl.multiple_of(j * width, width), width)
            out[:, cols] = act(left, weight, cols)
            return carry

        lax.fori_loop(0, out.shape[1] // width, tile, 0, unroll=True)

    def attention_out(self):
        self.tiles(self.acc, self.mixed, self.wo, lambda l, w, cols: dot_mid(l[...], w[:, cols]))
        for c in range(3):
            rows = slice(c * CHUNK, (c + 1) * CHUNK)
            hidden = self.x_rows(c) + (self.acc[rows, :] + self.branch[0:1, :])
            self.hidden[rows, :] = hidden
            self.norm_forward(hidden, 1, self.middle_t, c)

    def feed_up(self):
        root = 0.7978845608028654

        def tile(j, carry):
            cols = pl.ds(pl.multiple_of(j * TILE, TILE), TILE)
            x = dot_mid(self.normed[...], self.fc[:, cols]) + self.bias_up[0:1, cols]
            square = x * x
            half = 0.5 * jnp.tanh(x * (root + (0.044715 * root) * square)) + 0.5
            self.after[:, cols] = (x * half).astype(BF16)
            inner = x * (2.0 * root + (6.0 * 0.044715 * root) * square)
            self.before[:, cols] = (half + (half - half * half) * inner).astype(BF16)
            return carry

        lax.fori_loop(0, self.sizes.ff // TILE, tile, 0)

    def feed_down(self):
        self.tiles(self.acc, self.after, self.pt, lambda l, w, cols: dot_last(l[...], w[cols, :]))
        for c in range(3):
            rows = slice(c * CHUNK, (c + 1) * CHUNK)
            out = self.hidden[rows, :] + (self.acc[rows, :] + self.branch[1:2, :])
            self.cross[0, c] = out.astype(BF16)
            pl.when(self.section == 0)(lambda: self.cross_copy(c).start())

    def cross_copy(self, c):
        return self.remote(
            self.cross.at[self.section, c],
            self.land.at[1, c],
            self.cross_send.at[c],
            self.cross_recv.at[c],
            {"section": 1 - self.section},
        )

    def g_rows(self, c):
        return self.land[1 - self.section, c]

    def take_grad(self):
        for c in range(3):
            rows = slice(c * CHUNK, (c + 1) * CHUNK)
            self.normed[rows, :] = self.g_rows(c)
            self.grad_t[:, rows] = self.g_rows(c).T

    def feed_back(self):
        def tile(j, carry):
            cols = pl.ds(pl.multiple_of(j * TILE, TILE), TILE)
            grad = dot_mid(self.normed[...], self.pt[:, cols])
            self.before[:, cols] = (grad * self.before[:, cols].astype(F32)).astype(BF16)
            return carry

        lax.fori_loop(0, self.sizes.ff // TILE, tile, 0)
        self.tiles(self.acc, self.before, self.fc, lambda l, w, cols: dot_last(l[...], w[cols, :]))
        sums = [0.0, 0.0, 0.0, 0.0]
        for c in range(3):
            rows = slice(c * CHUNK, (c + 1) * CHUNK)
            grad = self.acc[rows, :]
            g = self.g_rows(c).astype(F32)
            unit, scale = norm_parts(self.hidden[rows, :])
            through = g + norm_back(grad, self.gains[1:2, :], unit, scale)
            self.grad_hidden[rows, :] = through
            low = through.astype(BF16)
            self.normed[rows, :] = low
            for a in range(NA):
                width = self.sizes.shard
                self.low_parts[a, rows, :] = low[:, a * width : (a + 1) * width]
            for i, value in enumerate((grad * unit, grad, through, g)):
                sums[i] = sums[i] + column_sum(value)
        self.vec[1:2, :] = sums[0]
        self.vec[3:4, :] = sums[1]
        self.vec[4:5, :] = sums[2]
        self.vec[5:6, :] = sums[3]
        dmodel = self.sizes.dmodel
        for part in range(self.sizes.ff // dmodel):
            self.vec[9 + part : 10 + part, :] = column_sum(
                self.before[:, part * dmodel : (part + 1) * dmodel].astype(F32)
            )

    def mixed_back(self):
        self.tiles(self.acc, self.normed, self.wo, lambda l, w, cols: dot_last(l[...], w[cols, :]))

    def inner_grad(self, j):
        cols = self.columns(j, 0)
        inverse = 1.0 / self.denom[:, cols]
        grad = self.acc[:, cols] * inverse
        return grad, -self.head_sum(grad * self.mixed[:, cols].astype(F32))

    def state_back(self):
        for c in range(3):
            self.state[c, self.sizes.state - 128 :, :] = jnp.zeros((128, 128), F32)

        def pair(j, carry):
            numers, denoms = self.inner_grad(j)
            for c in range(3):
                rows = slice(c * CHUNK, (c + 1) * CHUNK)
                usable = self.usable[c]
                outer = jnp.concatenate([numers[rows] * usable, denoms[rows] * usable], 1).astype(BF16)
                self.store_state(c, j, dot_first(self.qmap[j, rows, :], outer))
            return carry

        lax.fori_loop(0, self.sizes.heads // 2, pair, 0, unroll=UNROLL)

    def softmax_back(self, kind, grad):
        count = kind.shape[0]
        grad = jnp.concatenate([grad[:, 0:128], grad[:, 128:256]], 0)
        kind = jnp.concatenate([kind[:, 0:128], kind[:, 128:256]], 0).astype(F32)
        part = kind * (grad - self.head_sum(kind * grad))
        return (part[0:count] - part[count:]).astype(BF16)

    def attend_back(self, step=None):
        pairs = self.sizes.heads // 2
        place = lanes((CHUNK, 128))
        left = place < 64
        ones = jnp.where(left, 1.0, 0.0).astype(BF16)
        others = jnp.where(left, 0.0, 1.0).astype(BF16)
        single = jnp.where(place == 0, 1.0, 0.0).astype(BF16)
        double = jnp.where(place == 64, 1.0, 0.0).astype(BF16)
        corner = jnp.where(place % 64 == 0, 1.0, 0.0).astype(BF16)

        def pair(j, carry):
            cols = self.columns(j, 0)
            numers, denoms = self.inner_grad(j)
            numers, denoms = numers.astype(BF16), denoms.astype(BF16)
            grads_query = []
            for c in range(3):
                rows = slice(c * CHUNK, (c + 1) * CHUNK)
                numer, denom = numers[rows], denoms[rows]
                value = self.proj[rows, self.columns(j, 2)]
                query = self.qmap[j, rows, :]
                key = self.kmap[j, rows, :]
                mask = self.causal[c]
                usable = self.usable[c]
                both = jnp.concatenate([ones, ones], 1), jnp.concatenate([others, others], 1)
                inner = jnp.concatenate(
                    [
                        jnp.concatenate([numer * ones, denom * single], 1),
                        jnp.concatenate([numer * others, denom * double], 1),
                    ],
                    0,
                )
                grads = dot_last(inner, jnp.concatenate([value, jnp.ones_like(value)], 1))
                early = (grads[0:CHUNK] * mask).astype(BF16)
                late = (grads[CHUNK:] * mask).astype(BF16)
                grad_query = dot_mid(
                    jnp.concatenate([early, late], 1),
                    jnp.concatenate([key * both[0], key * both[1]], 0),
                )
                state = self.expand(self.enter, c, j)
                grads_query.append(
                    grad_query
                    + jnp.concatenate([usable, usable], 1)
                    * dot_last(jnp.concatenate([numer, denom * corner], 1), state)
                )
                grad_key = dot_first(
                    jnp.concatenate([early, late], 0),
                    jnp.concatenate([query * both[0], query * both[1]], 0),
                )
                scores = self.scores[j, rows, :]
                grad_value = dot_first(
                    jnp.concatenate([scores[:, 0:CHUNK], scores[:, CHUNK:]], 0),
                    jnp.concatenate([numer * ones, numer * others], 0),
                )
                self.acc[rows, cols] = grad_value
                self.denom[rows, cols] = grad_key[:, 0:128]
                self.hidden[rows, cols] = grad_key[:, 128:256]
            logits = self.softmax_back(self.qmap[j], jnp.concatenate(grads_query, 0))
            self.grad_maps[j] = dot_first(self.proj[:, cols], logits)
            self.proj[:, cols] = dot_last(logits, self.maps[j]).astype(BF16)
            if step is not None:
                step(j)
            return carry

        lax.fori_loop(0, pairs, pair, 0, unroll=UNROLL)

    def attend_back_keys(self):
        pairs = self.sizes.heads // 2
        corner = jnp.where(lanes((CHUNK, 128)) % 64 == 0, 1.0, 0.0).astype(BF16)

        def pair(j, carry):
            cols = self.columns(j, 0)
            grads_key = []
            for c in range(3):
                rows = slice(c * CHUNK, (c + 1) * CHUNK)
                kept = self.kept[c]
                value = self.proj[rows, self.columns(j, 2)]
                later = self.expand(self.later, c, j)
                grad_key = jnp.concatenate([self.denom[rows, cols], self.hidden[rows, cols]], 1)
                grads_key.append(
                    grad_key
                    + jnp.concatenate([kept, kept], 1)
                    * dot_last(jnp.concatenate([value, corner], 1), later)
                )
                grad_value = self.acc[rows, cols] + kept * dot_mid(self.kmap[j, rows, :], later[:, 0:128])
                self.proj[rows, self.columns(j, 2)] = grad_value.astype(BF16)
            logits = self.softmax_back(self.kmap[j], jnp.concatenate(grads_key, 0))
            self.grad_maps[pairs + j] = dot_first(self.proj[:, self.columns(j, 1)], logits)
            self.proj[:, self.columns(j, 1)] = dot_last(logits, self.maps[pairs + j]).astype(BF16)
            return carry

        lax.fori_loop(0, pairs, pair, 0, unroll=UNROLL)

    def project_back(self):
        self.tiles(self.acc, self.proj, self.wq, lambda l, w, cols: dot_last(l[...], w[cols, :]))
        sums = [0.0, 0.0]
        for c in range(3):
            rows = slice(c * CHUNK, (c + 1) * CHUNK)
            grad = self.acc[rows, :]
            unit, scale = norm_parts(self.x_rows(c))
            total = self.grad_hidden[rows, :] + norm_back(grad, self.gains[0:1, :], unit, scale)
            self.cross[1, c] = total.astype(BF16)
            pl.when(self.section == 1)(lambda: self.cross_copy(c).start())
            sums[0] = sums[0] + column_sum(grad * unit)
            sums[1] = sums[1] + column_sum(grad)
        self.vec[0:1, :] = sums[0]
        self.vec[2:3, :] = sums[1]
        dmodel = self.sizes.dmodel
        for part in range(3):
            self.vec[6 + part : 7 + part, :] = column_sum(
                self.proj[:, part * dmodel : (part + 1) * dmodel].astype(F32)
            )

    def partial(self, kind, a, z):
        s = self.sizes
        rows = pl.ds(pl.multiple_of(a * s.shard, 16), s.shard)
        cols = slice(z * s.ff_part, (z + 1) * s.ff_part)
        if kind == 2:
            return dot_mid(self.grad_t[rows, :], self.after[:, cols])
        if kind == 1:
            return dot_mid(self.middle_t[rows, :], self.before[:, cols])
        heads = s.heads // s.head
        width = heads * s.size
        pairs = s.heads // 2
        left = self.normed_t[rows, :]
        pieces = [
            dot_mid(left, self.proj[:, part * s.dmodel + z * width : part * s.dmodel + (z + 1) * width])
            for part in range(3)
        ]
        pieces.append(dot_first(self.mixed[:, z * width : (z + 1) * width], self.low_parts[a]))
        top = jnp.concatenate(pieces, 1)
        half = lanes((16, 128)) < 64
        blocks = []
        for k in range(2 * heads):
            head = heads * z + k // 2
            first = pl.multiple_of(64 * (head % 2) + 32 * (a % 2) + 16 * (k % 2), 16)
            block = self.grad_maps[(a // 2) * pairs + head // 2, pl.ds(first, 16), :]
            keep = half if head % 2 == 0 else jnp.logical_not(half)
            block = jnp.where(keep, block, 0.0)
            blocks.append(block + pltpu.roll(block, 64, 1))
        return jnp.concatenate([top, jnp.concatenate(blocks, 1)], 0)

    def first_slot(self, kind, index):
        if kind == 0:
            return self.pair_a.at[index]
        return self.slab.at[8 * (kind - 1) + index, pl.ds(0, self.sizes.shard)]

    def slot_rows(self, ref, index, kind):
        rows = self.sizes.shard + (16 if kind == 0 else 0)
        return ref.at[kind, index, pl.ds(0, rows)]

    def pair_copy(self, kind, index):
        rows = self.sizes.shard + (16 if kind == 0 else 0)
        return self.remote(
            self.stage.at[index, pl.ds(0, rows)],
            self.first_slot(kind, index),
            self.pair_send.at[kind, index],
            self.pair_recv.at[kind, index],
            self.towards(3),
        )

    def reduce_pair(self, kind):
        nz = self.sizes.head
        rows = self.sizes.shard + (16 if kind == 0 else 0)
        for near in range(2):
            y = self.y if near else 1 - self.y
            for z in self.outward:
                index = near * nz + z
                if kind != self.kinds[0]:
                    self.pair_copy(self.kinds[self.kinds.index(kind) - 1], index).wait_send()
                self.stage[index, 0:rows, :] = self.partial(kind, 2 * y + 1 - self.c, z).astype(BF16)
                self.pair_copy(kind, index).start()

    def across_copy(self, kind, z):
        return self.remote(
            self.first_slot(kind, z),
            self.slot_rows(self.across, z, kind),
            self.across_send.at[kind, z],
            self.across_recv.at[kind, z],
            self.towards(2),
        )

    def reduce_across(self, kind):
        for z in self.outward:
            self.pair_copy(kind, z).wait_recv()
            slot = self.first_slot(kind, z)
            total = self.partial(kind, 2 * (1 - self.y) + self.c, z) + slot[...].astype(F32)
            slot[...] = total.astype(BF16)
            self.across_copy(kind, z).start()

    def reduce_here(self, kind, places):
        nz = self.sizes.head
        for z in places:
            self.pair_copy(kind, nz + z).wait_recv()
            total = self.partial(kind, 2 * self.y + self.c, z) + self.first_slot(kind, nz + z)[...].astype(F32)
            self.across_copy(kind, z).wait_recv()
            slot = self.slot_rows(self.across, z, kind)
            slot[...] = (total + slot[...].astype(F32)).astype(BF16)
            pl.when(self.z != z)(lambda: self.line_copy(kind, z).start())

    def line_copy(self, kind, z):
        nz = self.sizes.head
        index = (self.z - z + nz) % nz - 1
        return self.remote(
            self.slot_rows(self.across, z, kind),
            self.slot_rows(self.line, jnp.maximum(index, 0), kind),
            self.line_send.at[kind, z],
            self.line_recv.at[kind, jnp.maximum(index, 0)],
            self.cell(self.a, z),
        )

    def reduce_last(self, kind):
        nz = self.sizes.head
        source, out = self.reduced(kind)
        total = self.slot_rows(self.across, self.z, kind)[...].astype(F32)
        for index in range(nz - 1):
            slot = self.slot_rows(self.line, index, kind)
            self.remote(
                slot, slot, self.line_send.at[kind, 0], self.line_recv.at[kind, index], self.cell(self.a, self.z)
            ).wait_recv()
            total = total + slot[...].astype(F32)
        source[...] = total
        pltpu.make_async_copy(source, out, self.reduced_send.at[kind]).start()

    def reduced(self, kind):
        shard = self.sizes.shard
        if kind == 0:
            return self.denom.at[pl.ds(0, shard + 16)], self.grad_a
        if kind == 1:
            return self.acc.at[pl.ds(0, shard)], self.grad_f
        return self.acc.at[pl.ds(shard, shard)], self.grad_p

    def reduce_end(self):
        nz = self.sizes.head
        for kind in self.kinds:
            source, out = self.reduced(kind)
            pltpu.make_async_copy(source, out, self.reduced_send.at[kind]).wait()
        for z in range(2 * nz):
            self.pair_copy(self.kinds[-1], z).wait_send()
        for kind in self.kinds:
            for z in range(nz):
                self.across_copy(kind, z).wait_send()
            for z in range(nz):
                pl.when(self.z != z)(lambda: self.line_copy(kind, z).wait_send())

    def vector_copy(self, stage):
        nz = self.sizes.head
        device = (
            self.towards(3),
            self.towards(2),
            self.cell(self.a, self.z + 1 - 2 * (self.z % 2)),
            self.cell(self.a, (self.z + nz // 2) % nz),
        )[stage]
        return self.remote(
            self.vec_out.at[stage],
            self.vec_in.at[stage],
            self.vec_send.at[stage],
            self.vec_recv.at[stage],
            device,
        )

    def vector_start(self, stage):
        self.vec_out[stage] = self.vec[...]
        self.vector_copy(stage).start()

    def vector_end(self, stage):
        self.vector_copy(stage).wait_recv()
        self.vec[...] = self.vec[...] + self.vec_in[stage]

    def run(self):
        nz = self.sizes.head
        self.kinds = (2, 1, 0)
        self.outward = [z for pair in zip(range(nz // 2), range(nz - 1, nz // 2 - 1, -1)) for z in pair]
        self.place()
        first = self.section == 0
        second = self.section == 1
        self.take_params()
        self.barrier()
        self.weight_own(0)
        self.deal()
        place = lax.broadcasted_iota(jnp.int32, (256, 128), 0) % 128 // 64
        self.ones[...] = jnp.where(place == lanes((256, 128)) // 64, 1.0, 0.0).astype(BF16)
        self.vec[...] = jnp.zeros_like(self.vec)
        start, steps, others, late = self.weight_steps()
        for step in start:
            step()

        @pl.when(second)
        def _():
            for step in others:
                step()
            for d in range(nz):
                self.relay(d, True)

        at = [0]

        def some_weights(number):
            taken = steps[at[0] : at[0] + number]
            at[0] += number

            @pl.when(first)
            def _():
                for step in taken:
                    step()

        self.assemble()
        self.dealt()
        self.masks()
        some_weights(2)
        for c in range(3):
            pl.when(second)(lambda: self.cross_copy(c).wait_recv())
        self.project()
        some_weights(1)

        def between(j):
            for k in range(3):

                @pl.when(first & (j == 2 * k + 1))
                def _():
                    steps[at[0] + k]()

        self.map_keys(between)
        at[0] += 3
        self.chain_start(True)
        self.map_queries()
        n = self.n
        count = self.sizes.heads // 2
        depth = self.p - ((3 * self.p) // n * n) // 3
        when = jnp.clip(5 * (depth - 1) // 2, 0, count - 1)

        def meanwhile(j):
            for k in range(count):
                pl.when(first & (j == k))(steps[at[0] + k])
            pl.when(j == when)(lambda: self.chain_pass(True))

        self.attend_inner(meanwhile)
        at[0] += count
        pl.when(second)(late[0])
        self.attend_outer()
        some_weights(1)
        pl.when(second)(late[1])
        self.attention_out()
        some_weights(2)
        pl.when(second)(late[2])
        self.feed_up()
        some_weights(len(steps))

        @pl.when(second)
        def _():
            for step in late[3:]:
                step()

        self.weight_end(0)
        pl.semaphore_signal(self.free, inc=1, device_id=self.towards(3), device_id_type=MESH)
        self.feed_down()

        @pl.when(first)
        def _():
            self.send_home(0)
            for c in range(3):
                self.cross_copy(c).wait_recv()

        self.take_grad()

        @pl.when(first)
        def _():
            pl.semaphore_wait(self.free, 1)
            self.reduce_pair(2)
            self.reduce_across(2)

        self.feed_back()

        hold = self.p % (2 * nz) < 2
        pl.when(first)(lambda: self.reduce_pair(1))
        self.mixed_back()
        self.state_back()
        self.chain_start(False)
        pl.when(first & jnp.logical_not(hold))(lambda: self.reduce_across(1))
        n = self.n
        depth = (((3 * self.p + 2) // n + 1) * n - 1) // 3 - self.p
        when = jnp.minimum(jnp.maximum(2 * depth - 2, 0), self.sizes.heads // 2 - 1)

        def during(j):
            pl.when(j == when)(lambda: self.chain_pass(False))

        self.attend_back(during)

        pl.when(first & hold)(lambda: self.reduce_across(1))
        pl.when(first)(lambda: self.reduce_here(2, self.outward))
        self.attend_back_keys()
        self.project_back()

        self.vector_start(0)

        @pl.when(second)
        def _():
            pl.semaphore_wait(self.free, 1)
            self.reduce_pair(2)
            self.reduce_across(2)
            self.reduce_pair(1)
            self.reduce_across(1)

        self.reduce_pair(0)
        self.vector_end(0)
        self.vector_start(1)
        self.reduce_across(0)
        pl.when(second)(lambda: self.send_home(0))
        self.send_home(1)
        pl.when(second)(lambda: self.reduce_here(2, self.outward))
        self.vector_end(1)
        self.vector_start(2)
        self.reduce_here(1, self.outward)
        self.vector_end(2)
        self.vector_start(3)
        self.reduce_last(2)
        self.reduce_here(0, self.outward)
        self.reduce_last(1)
        self.vector_end(3)
        self.reduce_last(0)
        for stage in range(4):
            self.vector_copy(stage).wait_send()
        self.grad_gains[...] = self.vec[0:2, :]
        self.grad_biases[...] = self.vec[2:4, :]
        self.grad_branch[...] = self.vec[4:6, :]
        self.grad_bias_in[...] = self.vec[6:9, :]
        dmodel = self.sizes.dmodel
        for part in range(self.sizes.ff // dmodel):
            self.grad_bias_up[:, part * dmodel : (part + 1) * dmodel] = self.vec[9 + part : 10 + part, :]
        self.deal_end()
        self.weight_end(1)
        self.weight_end(2)
        for c in range(3):
            self.cross_copy(c).wait_send()
        self.chain_end(True)
        self.chain_end(False)
        self.reduce_end()
        self.home_end(0)
        self.home_end(1)


def scratch(s):
    rows, dmodel, ff, shard = 3 * CHUNK, s.dmodel, s.ff, s.shard
    pairs, nz, state = s.heads // 2, s.head, s.state
    vmem, dma = pltpu.VMEM, pltpu.SemaphoreType.DMA
    cells = NA * nz
    return dict(
        seg_in=vmem((3, 8, CHUNK), F32),
        gains=vmem((2, dmodel), F32),
        biases=vmem((2, dmodel), F32),
        branch=vmem((2, dmodel), F32),
        bias_in=vmem((3, dmodel), F32),
        bias_up=vmem((1, ff), F32),
        vec=vmem((16, dmodel), F32),
        land=vmem((2, 3, CHUNK, dmodel), BF16),
        segs=vmem((3, 8, CHUNK), F32),
        slab=vmem((cells, shard + 16, dmodel), BF16),
        fc=vmem((dmodel, ff), BF16),
        pt=vmem((dmodel, ff), BF16),
        wq=vmem((dmodel, 3 * dmodel), BF16),
        wo=vmem((dmodel, dmodel), BF16),
        maps=vmem((2 * pairs, 128, 128), BF16),
        ones=vmem((256, 128), BF16),
        causal=vmem((3, CHUNK, CHUNK), F32),
        usable=vmem((3, CHUNK, CHUNK), F32),
        kept=vmem((3, CHUNK, CHUNK), F32),
        normed=vmem((rows, dmodel), BF16),
        normed_t=vmem((dmodel, rows), BF16),
        middle_t=vmem((dmodel, rows), BF16),
        grad_t=vmem((dmodel, rows), BF16),
        proj=vmem((rows, 3 * dmodel), BF16),
        qmap=vmem((pairs, rows, 256), BF16),
        kmap=vmem((pairs, rows, 256), BF16),
        scores=vmem((pairs, rows, 256), BF16),
        denom=vmem((rows, dmodel), F32),
        mixed=vmem((rows, dmodel), BF16),
        acc=vmem((rows, dmodel), F32),
        hidden=vmem((rows, dmodel), F32),
        grad_hidden=vmem((rows, dmodel), F32),
        after=vmem((rows, ff), BF16),
        before=vmem((rows, ff), BF16),
        low_parts=vmem((NA, rows, shard), BF16),
        cross=vmem((2, 3, CHUNK, dmodel), BF16),
        state=vmem((3, state, 128), F32),
        chain_own=vmem((state, 128), F32),
        enter=vmem((3, state, 128), BF16),
        later=vmem((3, state, 128), BF16),
        message=vmem((state, 128), BF16),
        landed=vmem((state, 128), BF16),
        message_back=vmem((state, 128), BF16),
        landed_back=vmem((state, 128), BF16),
        grad_maps=vmem((2 * pairs, 128, 128), F32),
        stage=vmem((2 * nz, shard + 16, dmodel), BF16),
        pair_a=vmem((2 * nz, shard + 16, dmodel), BF16),
        across=vmem((3, nz, shard + 16, dmodel), BF16),
        line=vmem((3, nz - 1, shard + 16, dmodel), BF16),
        vec_out=vmem((4, 16, dmodel), F32),
        vec_in=vmem((4, 16, dmodel), F32),
        deal_send=dma((3,)),
        deal_recv=dma((3,)),
        segs_send=dma((3,)),
        segs_recv=dma((3,)),
        ag_send=dma((3, 4, cells)),
        ag_recv=dma((3, cells)),
        ag_own=dma((3,)),
        relay_send=dma((nz,)),
        relay_recv=dma((nz,)),
        cross_send=dma((3,)),
        cross_recv=dma((3,)),
        chain_send=dma((2,)),
        chain_recv=dma((2,)),
        home_send=dma((2, 3)),
        home_recv=dma((2, 3)),
        pair_send=dma((3, 2 * nz)),
        pair_recv=dma((3, 2 * nz)),
        across_send=dma((3, nz)),
        across_recv=dma((3, nz)),
        line_send=dma((3, nz)),
        line_recv=dma((3, nz - 1)),
        reduced_send=dma((3,)),
        vec_send=dma((4,)),
        vec_recv=dma((4,)),
        free=pltpu.SemaphoreType.REGULAR,
    )


def train_step(s, *args):
    held = scratch(s)
    anywhere = pl.BlockSpec(memory_space=pl.ANY)
    inside = pl.BlockSpec(memory_space=pltpu.VMEM)
    dmodel, shard = s.dmodel, s.shard
    given = dict(
        x_in=anywhere,
        g_in=anywhere,
        seg_ids=inside,
        sh_a=anywhere,
        sh_f=anywhere,
        sh_p=anywhere,
        gains_in=inside,
        biases_in=inside,
        branch_in=inside,
        bias_in_in=inside,
        bias_up_in=inside,
    )
    made = dict(
        out_rows=anywhere,
        grad_rows=anywhere,
        grad_a=anywhere,
        grad_f=anywhere,
        grad_p=anywhere,
        grad_gains=inside,
        grad_biases=inside,
        grad_branch=inside,
        grad_bias_in=inside,
        grad_bias_up=inside,
    )
    names = list(given) + list(made) + list(held)

    def body(*refs):
        Step(s, names, refs).run()

    return pl.pallas_call(
        body,
        out_shape=(
            jax.ShapeDtypeStruct((3, CHUNK, dmodel), BF16),
            jax.ShapeDtypeStruct((3, CHUNK, dmodel), BF16),
            jax.ShapeDtypeStruct((shard + 16, dmodel), F32),
            jax.ShapeDtypeStruct((shard, dmodel), F32),
            jax.ShapeDtypeStruct((shard, dmodel), F32),
            jax.ShapeDtypeStruct((2, dmodel), F32),
            jax.ShapeDtypeStruct((2, dmodel), F32),
            jax.ShapeDtypeStruct((2, dmodel), F32),
            jax.ShapeDtypeStruct((3, dmodel), F32),
            jax.ShapeDtypeStruct((1, s.ff), F32),
        ),
        in_specs=list(given.values()),
        out_specs=tuple(made.values()),
        scratch_shapes=list(held.values()),
        compiler_params=pltpu.CompilerParams(
            collective_id=0, has_side_effects=True, vmem_limit_bytes=64 * 1024 * 1024
        ),
        name="train_step",
    )(*args)


def local(
    block_input,
    segment_ids,
    output_grad,
    norm_gains,
    norm_biases,
    qkv_weight,
    qkv_bias,
    feature_maps,
    out_weight,
    branch_bias,
    fc_weight,
    fc_bias,
    proj_weight,
):
    nt, nz = lax.axis_size("tok"), lax.axis_size("head")
    micro, rows, dmodel = block_input.shape
    heads = feature_maps.shape[1] * nz
    ff = fc_bias.shape[1]
    size = dmodel // heads
    group = nt // NA
    sizes = Sizes(
        tok=nt,
        head=nz,
        micro=micro,
        dmodel=dmodel,
        heads=heads,
        size=size,
        ff=ff,
        ff_part=ff // nz,
        shard=dmodel // NA,
        state=heads // 2 * 128 + 128,
    )
    assert micro == 3 and rows == CHUNK and size == 64 and nt % NA == 0
    groups = [[group * a + b for b in range(group)] for a in range(NA)]

    def widen(part, dim):
        if group == 1:
            return part
        return lax.all_gather(part, "tok", axis=dim, tiled=True, axis_index_groups=groups)

    def narrow(part, dim):
        if group == 1:
            return part
        return lax.psum_scatter(part, "tok", scatter_dimension=dim, tiled=True, axis_index_groups=groups)

    shard = dmodel // NA
    width = dmodel // nz
    w_in = widen(qkv_weight[0], 0).reshape(shard, 3 * width)
    w_out = widen(out_weight[0], 1)
    maps = widen(feature_maps[0], 1)
    w_up = widen(fc_weight[0], 0)
    w_down = widen(proj_weight[0], 1).T
    maps = maps.reshape(2 * heads // nz, 16, size)
    maps = jnp.concatenate([maps, maps], 2).transpose(1, 0, 2).reshape(16, 4 * heads // nz * size)
    sh_a = jnp.concatenate([jnp.concatenate([w_in, w_out], 1), maps], 0)
    out_rows, grad_rows, grad_a, grad_f, grad_p, *vectors = train_step(
        sizes,
        block_input,
        output_grad,
        segment_ids,
        sh_a,
        w_up,
        w_down,
        norm_gains[0],
        norm_biases[0],
        branch_bias[0],
        qkv_bias[0],
        fc_bias,
    )
    if group > 1:
        vectors = [jnp.sum(lax.all_gather(v, "tok", axis=0, axis_index_groups=groups), 0) for v in vectors]
    grad_in = narrow(grad_a[:shard, : 3 * width].reshape(shard, 3, width), 0)
    grad_out = narrow(grad_a[:shard, 3 * width :], 1)
    grad_maps = grad_a[shard:].reshape(16, 2 * heads // nz, 2 * size)[:, :, :size]
    grad_maps = narrow(grad_maps.transpose(1, 0, 2).reshape(heads // nz, 2 * 16 * size), 1)
    return (
        out_rows[None].astype(F32),
        grad_rows[None].astype(F32),
        vectors[0][None],
        vectors[1][None],
        grad_in[None],
        vectors[3][None],
        grad_maps[None],
        grad_out[None],
        vectors[2][None],
        narrow(grad_f, 0)[None],
        vectors[4],
        narrow(grad_p, 0).T[None],
    )


def solution(mesh):
    in_specs = (
        P(None, ("tok", "head"), None),
        P(None, "tok"),
        P(None, ("tok", "head"), None),
        P("section", None, None),
        P("section", None, None),
        P("section", "tok", None, "head"),
        P("section", None, None),
        P("section", "head", "tok"),
        P("section", "head", "tok"),
        P("section", None, None),
        P("section", "tok", "head"),
        P("section", None),
        P("section", "head", "tok"),
    )
    out_specs = (
        P("section", None, ("tok", "head"), None),
        P("section", None, ("tok", "head"), None),
        P("section", None, None),
        P("section", None, None),
        P("section", "tok", None, "head"),
        P("section", None, None),
        P("section", "head", "tok"),
        P("section", "head", "tok"),
        P("section", None, None),
        P("section", "tok", "head"),
        P("section", None),
        P("section", "head", "tok"),
    )
    return jax.shard_map(local, mesh=mesh, in_specs=in_specs, out_specs=out_specs, check_vma=False)
```

```python
import functools
import typing

import jax
import jax.numpy as jnp
from jax import lax
from jax.experimental import pallas as pl
from jax.experimental.pallas import tpu as pltpu
from jax.sharding import PartitionSpec as P

MESH = pl.DeviceIdType.MESH
EPS = 1e-05
F32 = jnp.float32
BF16 = jnp.bfloat16
NA = 4
CHUNK = 128
TILE = 768
UNROLL = 6


def dot_mid(left, right):
    return lax.dot_general(left, right, (((1,), (0,)), ((), ())), preferred_element_type=F32)


def dot_last(left, right):
    return lax.dot_general(left, right, (((1,), (1,)), ((), ())), preferred_element_type=F32)


def dot_first(left, right):
    return lax.dot_general(left, right, (((0,), (0,)), ((), ())), preferred_element_type=F32)


def norm_parts(rows):
    center = jnp.mean(rows, -1, keepdims=True)
    centred = rows - center
    spread = jnp.mean(centred * centred, -1, keepdims=True)
    scale = lax.rsqrt(spread + EPS)
    return centred * scale, scale


def norm_back(grad, gain, unit, scale):
    inner = grad * gain
    first = jnp.mean(inner, -1, keepdims=True)
    second = jnp.mean(inner * unit, -1, keepdims=True)
    return scale * (inner - first - unit * second)


def lanes(shape):
    return lax.broadcasted_iota(jnp.int32, shape, len(shape) - 1)


def column_sum(value):
    return jnp.sum(value, 0, keepdims=True)


class Sizes(typing.NamedTuple):
    tok: int
    head: int
    micro: int
    dmodel: int
    heads: int
    size: int
    ff: int
    ff_part: int
    shard: int
    state: int


class Step:
    def __init__(self, sizes, names, refs):
        self.sizes = sizes
        for name, ref in zip(names, refs):
            setattr(self, name, ref)

    def place(self):
        s = self.sizes
        self.section = lax.axis_index("section")
        self.tok = lax.axis_index("tok")
        self.z = lax.axis_index("head")
        group = s.tok // NA
        self.a = self.tok // group
        self.b = self.tok % group
        self.group = group
        self.y = self.a // 2
        self.c = self.a % 2
        self.n = s.tok * s.head
        self.home = self.tok * s.head + self.z
        r, core = self.tok // 2, self.tok % 2
        k = jnp.where(r % 2 == 0, self.z, s.head - 1 - self.z)
        self.p = r * (2 * s.head) + 2 * k + core

    def device_of_place(self, p):
        nz = self.sizes.head
        r = p // (2 * nz)
        k = (p % (2 * nz)) // 2
        z = jnp.where(r % 2 == 0, k, nz - 1 - k)
        return 2 * r + p % 2, z

    def cell(self, a, z):
        return {"tok": a * self.group + self.b, "head": z}

    def remote(self, src, dst, send, recv, device):
        return pltpu.make_async_remote_copy(
            src_ref=src, dst_ref=dst, send_sem=send, recv_sem=recv, device_id=device, device_id_type=MESH
        )

    def barrier(self):
        nt, nz = self.sizes.tok, self.sizes.head
        sem = pltpu.get_barrier_semaphore()

        def greet(k, carry):
            other = lax.rem(self.home + k, nt * nz)
            pl.semaphore_signal(
                sem,
                inc=1,
                device_id={"tok": other // nz, "head": other % nz},
                device_id_type=MESH,
            )
            return carry

        lax.fori_loop(1, nt * nz, greet, 0)
        pl.semaphore_signal(sem, inc=1, device_id={"section": 1 - self.section}, device_id_type=MESH)
        pl.semaphore_signal(sem, inc=1, device_id=self.corner(), device_id_type=MESH)
        pl.semaphore_wait(sem, nt * nz + 1)

    def take_params(self):
        for wide, ref in (
            (self.gains, self.gains_in),
            (self.biases, self.biases_in),
            (self.branch, self.branch_in),
            (self.bias_in, self.bias_in_in),
            (self.bias_up, self.bias_up_in),
        ):
            wide[...] = ref[...].astype(F32)
        here = pl.ds(pl.multiple_of(self.z * CHUNK, CHUNK), CHUNK)
        ahead = pl.ds(pl.multiple_of(jnp.maximum(self.z - 1, 0) * CHUNK, CHUNK), CHUNK)
        row = lax.broadcasted_iota(jnp.int32, (8, CHUNK), 0)
        for m in range(self.sizes.micro):
            ids = self.seg_ids[m : m + 1, here].astype(F32)
            before = self.seg_ids[m : m + 1, ahead].astype(F32)[:, CHUNK - 1 :]
            before = jnp.where(self.z > 0, before, jnp.where(self.tok > 0, 2.0, -1.0))
            self.seg_in[m] = jnp.where(row == 0, ids, jnp.where(row == 1, before, ids[:, CHUNK - 1 :]))

    def deal(self):
        for m in range(self.sizes.micro):
            q = self.n * m + self.home
            p, slot = q // 3, q % 3
            tok, z = self.device_of_place(p)
            here = p == self.p
            device = {"tok": tok, "head": z}

            @pl.when(here)
            def _():
                pltpu.make_async_copy(self.seg_in.at[m], self.segs.at[slot], self.segs_recv.at[slot]).start()

            @pl.when(jnp.logical_not(here))
            def _():
                self.remote(
                    self.seg_in.at[m], self.segs.at[slot], self.segs_send.at[m], self.segs_recv.at[slot], device
                ).start()

            for section, rows in enumerate((self.x_in, self.g_in)):
                mine = self.section == section

                @pl.when(mine & here)
                def _():
                    pltpu.make_async_copy(rows.at[m], self.land.at[0, slot], self.deal_recv.at[slot]).start()

                @pl.when(mine & jnp.logical_not(here))
                def _():
                    self.remote(
                        rows.at[m], self.land.at[0, slot], self.deal_send.at[m], self.deal_recv.at[slot], device
                    ).start()

    def dealt(self):
        for slot in range(3):
            q = 3 * self.p + slot
            here = q % self.n == self.home

            @pl.when(here)
            def _():
                pltpu.make_async_copy(self.x_in.at[0], self.land.at[0, slot], self.deal_recv.at[slot]).wait()
                pltpu.make_async_copy(self.seg_in.at[0], self.segs.at[slot], self.segs_recv.at[slot]).wait()

            @pl.when(jnp.logical_not(here))
            def _():
                device = {"tok": self.tok, "head": self.z}
                self.remote(
                    self.seg_in.at[0], self.segs.at[slot], self.segs_send.at[0], self.segs_recv.at[slot], device
                ).wait_recv()
                self.remote(
                    self.x_in.at[0], self.land.at[0, slot], self.deal_send.at[0], self.deal_recv.at[slot], device
                ).wait_recv()

    def deal_end(self):
        for m in range(self.sizes.micro):
            q = self.n * m + self.home

            @pl.when(q // 3 != self.p)
            def _():
                device = {"tok": self.tok, "head": self.z}
                self.remote(
                    self.seg_in.at[m], self.segs.at[0], self.segs_send.at[m], self.segs_recv.at[0], device
                ).wait_send()
                self.remote(
                    self.x_in.at[m], self.land.at[0, 0], self.deal_send.at[m], self.deal_recv.at[0], device
                ).wait_send()

    def send_home(self, index):
        out = (self.out_rows, self.grad_rows)[index]
        nz = self.sizes.head
        for slot in range(3):
            q = 3 * self.p + slot
            m, home = q // self.n, q % self.n
            here = home == self.home
            rows = self.cross.at[index, slot]
            recv = self.home_recv.at[index, m]

            @pl.when(here)
            def _():
                pltpu.make_async_copy(rows, out.at[m], recv).start()

            @pl.when(jnp.logical_not(here))
            def _():
                self.remote(
                    rows, out.at[m], self.home_send.at[index, slot], recv, {"tok": home // nz, "head": home % nz}
                ).start()

    def home_end(self, index):
        out = (self.out_rows, self.grad_rows)[index]
        device = {"tok": self.tok, "head": self.z}
        for slot in range(3):

            @pl.when((3 * self.p + slot) % self.n != self.home)
            def _():
                self.remote(
                    self.cross.at[index, slot],
                    out.at[0],
                    self.home_send.at[index, slot],
                    self.home_recv.at[index, 0],
                    device,
                ).wait_send()

        for m in range(self.sizes.micro):
            here = (self.n * m + self.home) // 3 == self.p
            recv = self.home_recv.at[index, m]

            @pl.when(here)
            def _():
                pltpu.make_async_copy(self.cross.at[index, 0], out.at[m], recv).wait()

            @pl.when(jnp.logical_not(here))
            def _():
                self.remote(
                    self.cross.at[index, 0], out.at[m], self.home_send.at[index, 0], recv, device
                ).wait_recv()

    def region(self, kind, a, z):
        s = self.sizes
        if kind == 0:
            return self.slab.at[a * s.head + z]
        full = self.fc if kind == 1 else self.pt
        rows, cols = s.shard, s.ff_part
        return full.at[pl.ds(pl.multiple_of(a * rows, 16), rows), pl.ds(pl.multiple_of(z * cols, 128), cols)]

    def towards(self, way):
        if way == 0:
            return self.cell(self.a, self.z + 1)
        if way == 1:
            return self.cell(self.a, self.z - 1)
        if way == 2:
            return self.cell(2 * (1 - self.y) + self.c, self.z)
        return self.cell(2 * self.y + 1 - self.c, self.z)

    def weight_copy(self, kind, a, z, way, own):
        s = self.sizes
        origin = a * s.head + z
        source = (self.sh_a, self.sh_f, self.sh_p)[kind] if own else self.region(kind, a, z)
        return self.remote(
            source,
            self.region(kind, a, z),
            self.ag_send.at[kind, way, origin],
            self.ag_recv.at[kind, origin],
            self.towards(way),
        )

    def corner(self):
        return {"section": 1 - self.section, **self.towards(2)}

    def relay_slot(self, z):
        s = self.sizes
        return self.after.at[pl.ds(0, s.shard), pl.ds(pl.multiple_of(z * s.ff_part, 128), s.ff_part)]

    def relay_in(self, z, own):
        return self.remote(
            self.sh_p if own else self.region(2, self.a, z),
            self.relay_slot(z),
            self.ag_send.at[2, 2, self.a * self.sizes.head + z],
            self.relay_recv.at[z],
            self.corner(),
        )

    def relay_out(self, z):
        a = 2 * (1 - self.y) + self.c
        return self.remote(
            self.relay_slot(z),
            self.region(2, a, z),
            self.relay_send.at[z],
            self.ag_recv.at[2, a * self.sizes.head + z],
            {"section": 1 - self.section},
        )

    def relay(self, d, end=False):
        for sign in (-1, 1) if d else (1,):
            z = self.z + sign * d

            @pl.when((z >= 0) & (z < self.sizes.head))
            def _():
                if end:
                    self.relay_out(z).wait_send()
                else:
                    self.relay_in(z, False).wait_recv()
                    self.relay_out(z).start()

    def weight_sends(self, kind, a, z, ways, own, act):
        for way in ways:
            if kind == 2 and way == 2:
                pl.when(self.section == 0)(lambda: act(self.relay_in(z, own)))
                pl.when(self.section == 1)(lambda: act(self.weight_copy(kind, a, z, 2, own)))
            elif way == 0:
                pl.when(self.z < self.sizes.head - 1)(lambda: act(self.weight_copy(kind, a, z, 0, own)))
            elif way == 1:
                pl.when(self.z > 0)(lambda: act(self.weight_copy(kind, a, z, 1, own)))
            else:
                act(self.weight_copy(kind, a, z, way, own))

    def weight_own(self, kind):
        source = (self.sh_a, self.sh_f, self.sh_p)[kind]
        self.weight_sends(kind, self.a, self.z, (2, 0, 1, 3), True, lambda copy: copy.start())
        pltpu.make_async_copy(source, self.region(kind, self.a, self.z), self.ag_own.at[kind]).start()

    def weight_line(self, kind, d, act=None):
        start = act is None
        for sign, way in ((-1, 0), (1, 1)):
            z = self.z + sign * d
            inside = z >= 0 if sign < 0 else z < self.sizes.head

            @pl.when(inside)
            def _():
                if start:
                    self.weight_copy(kind, self.a, z, 3, False).wait_recv()
                self.weight_sends(
                    kind, self.a, z, (2, way, 3), False, (lambda copy: copy.start()) if start else act
                )

    def weight_cross(self, kind, d, act=None):
        start = act is None
        a = 2 * (1 - self.y) + self.c
        for sign in (-1, 1) if d else (1,):
            z = self.z + sign * d
            inside = (z >= 0) & (z < self.sizes.head)

            @pl.when(inside)
            def _():
                copy = self.weight_copy(kind, a, z, 3, False)
                if start:
                    copy.wait_recv()
                    copy.start()
                else:
                    act(copy)

    def weight_last(self, kind):
        for y in range(2):
            for z in range(self.sizes.head):
                self.weight_copy(kind, 2 * y + 1 - self.c, z, 3, False).wait_recv()
        source = (self.sh_a, self.sh_f, self.sh_p)[kind]
        pltpu.make_async_copy(source, self.region(kind, self.a, self.z), self.ag_own.at[kind]).wait()

    def weight_steps(self):
        nz = self.sizes.head
        line = lambda kind, d: functools.partial(self.weight_line, kind, d)
        cross = lambda kind, d: functools.partial(self.weight_cross, kind, d)
        own = lambda kind: functools.partial(self.weight_own, kind)
        last = lambda kind: functools.partial(self.weight_last, kind)
        relay = lambda d: functools.partial(self.relay, d)
        start = [line(0, 1), own(1)] + [line(0, d) for d in range(2, nz)]
        start += [cross(0, d) for d in range(nz)] + [last(0)]
        one = [line(1, 1), own(2)] + [line(1, d) for d in range(2, nz)] + [cross(1, 0)]
        for d in range(1, nz):
            one += [cross(1, d), line(2, d)]
        one += [last(1)] + [cross(2, d) for d in range(nz)] + [last(2)]
        two = [line(1, 1), own(2)] + [line(1, d) for d in range(2, nz)]
        for d in range(nz):
            two += [relay(d), cross(1, d)]
        two += [last(1)] + [line(2, d) for d in range(1, nz)]
        return start, one, two, [cross(2, d) for d in range(nz)] + [last(2)]

    def weight_end(self, kind):
        nz = self.sizes.head
        finish = lambda copy: copy.wait_send()
        self.weight_sends(kind, self.a, self.z, (2, 0, 1, 3), True, finish)
        for d in range(1, nz):
            self.weight_line(kind, d, finish)
        for d in range(nz):
            self.weight_cross(kind, d, finish)

    def assemble(self):
        s = self.sizes
        nz, rows, heads = s.head, s.shard, s.heads // s.head
        width = heads * s.size
        dmodel = s.dmodel
        half = lanes((16, 128)) < 64
        for a in range(NA):
            for part in range(3):
                self.wq[a * rows : (a + 1) * rows, part * dmodel : (part + 1) * dmodel] = jnp.concatenate(
                    [self.slab[a * nz + z, 0:rows, part * width : (part + 1) * width] for z in range(nz)], 1
                )
        for z in range(nz):
            self.wo[z * width : (z + 1) * width, :] = jnp.concatenate(
                [self.slab[a * nz + z, 0:rows, 3 * width : 3 * width + rows] for a in range(NA)], 1
            )
        pairs = s.heads // 2
        for a in range(NA):
            for z in range(nz):
                for k in range(2 * heads):
                    head = heads * z + k // 2
                    block = self.slab[a * nz + z, rows : rows + 16, 128 * k : 128 * k + 128]
                    keep = half if head % 2 == 0 else jnp.logical_not(half)
                    first = 64 * (head % 2) + 32 * (a % 2) + 16 * (k % 2)
                    self.maps[(a // 2) * pairs + head // 2, first : first + 16, :] = jnp.where(
                        keep, block, jnp.zeros_like(block)
                    )

    def masks(self):
        for c in range(3):
            tile = self.segs[c]
            row = jnp.broadcast_to(tile[0:1], (CHUNK, CHUNK))
            column = row.T
            order = lax.broadcasted_iota(jnp.int32, (CHUNK, CHUNK), 0) >= lanes((CHUNK, CHUNK))
            self.causal[c] = jnp.where(order & (row == column), 1.0, 0.0)
            self.usable[c] = jnp.where(column == tile[1:2], 1.0, 0.0)
            self.kept[c] = jnp.where(column == tile[2:3], 1.0, 0.0)

    def linked(self, c):
        tile = self.segs[c]
        return jnp.where(tile[1:2] == tile[2:3], 1.0, 0.0)

    def head_sum(self, value):
        high = value.astype(BF16)
        low = (value - high.astype(F32)).astype(BF16)
        return dot_mid(jnp.concatenate([high, low], 1), self.ones[...])

    def norm_forward(self, rows, index, transposed, c):
        unit, _ = norm_parts(rows)
        low = (unit * self.gains[index : index + 1, :] + self.biases[index : index + 1, :]).astype(BF16)
        self.normed[c * CHUNK : (c + 1) * CHUNK, :] = low
        transposed[:, c * CHUNK : (c + 1) * CHUNK] = low.T

    def x_rows(self, c):
        return self.land[self.section, c].astype(F32)

    def project(self):
        s = self.sizes
        for c in range(3):
            self.norm_forward(self.x_rows(c), 0, self.normed_t, c)

        def tile(j, carry):
            cols = pl.ds(pl.multiple_of(j * TILE, TILE), TILE)
            value = dot_mid(self.normed[...], self.wq[:, cols]) + self.bias_in[pl.ds(j, 1), :]
            self.proj[:, cols] = value.astype(BF16)
            return carry

        lax.fori_loop(0, 3 * s.dmodel // TILE, tile, 0)

    def features(self, logits):
        left = lanes(logits.shape) < 64
        infinity = jnp.float32(jnp.inf)
        top = jnp.where(
            left,
            jnp.max(jnp.where(left, logits, -infinity), -1, keepdims=True),
            jnp.max(jnp.where(left, -infinity, logits), -1, keepdims=True),
        )
        bottom = jnp.where(
            left,
            jnp.min(jnp.where(left, logits, infinity), -1, keepdims=True),
            jnp.min(jnp.where(left, infinity, logits), -1, keepdims=True),
        )
        up = jnp.exp(logits - top)
        down = jnp.exp(bottom - logits)
        both = jnp.concatenate([up, down], 0)
        both = both / dot_mid(both.astype(BF16), self.ones[0:128, :])
        count = logits.shape[0]
        return jnp.concatenate([both[0:count], both[count:]], 1).astype(BF16)

    def columns(self, j, part):
        return pl.ds(pl.multiple_of(part * self.sizes.dmodel + j * 128, 128), 128)

    def compact(self, full):
        left = lanes((64, 128)) < 64
        return jnp.concatenate(
            [jnp.where(left, full[0:64], full[64:128]), jnp.where(left, full[128:192], full[192:256])], 0
        )

    def store_state(self, c, j, full):
        nrow = self.sizes.state - 128
        self.state[c, pl.ds(pl.multiple_of(j * 128, 128), 128), :] = self.compact(full[:, 0:128])
        norms = self.compact(full[:, 128:256])
        pick = lanes((128, 128)) % 64 == j
        self.state[c, nrow : nrow + 128, :] = jnp.where(pick, norms, self.state[c, nrow : nrow + 128, :])

    def expand(self, held, c, j):
        nrow = self.sizes.state - 128
        left = lanes((64, 128)) < 64
        zero = jnp.zeros((64, 128), F32)
        values = held[c, pl.ds(pl.multiple_of(j * 128, 128), 128), :].astype(F32)
        norms = held[c, nrow : nrow + 128, :].astype(F32)
        place = lanes((128, 128))
        norms = jnp.where(
            place < 64,
            jnp.sum(jnp.where(place == j, norms, 0.0), -1, keepdims=True),
            jnp.sum(jnp.where(place == 64 + j, norms, 0.0), -1, keepdims=True),
        )

        def spread(tile):
            up, down = tile[0:64], tile[64:128]
            return jnp.concatenate(
                [
                    jnp.where(left, up, zero),
                    jnp.where(left, zero, up),
                    jnp.where(left, down, zero),
                    jnp.where(left, zero, down),
                ],
                0,
            )

        return jnp.concatenate([spread(values), spread(norms)], 1).astype(BF16)

    def map_keys(self, step=None):
        pairs = self.sizes.heads // 2
        for c in range(3):
            self.state[c, self.sizes.state - 128 :, :] = jnp.zeros((128, 128), F32)

        def pair(j, carry):
            self.kmap[j] = self.features(dot_mid(self.proj[:, self.columns(j, 1)], self.maps[pairs + j]))
            for c in range(3):
                rows = slice(c * CHUNK, (c + 1) * CHUNK)
                kept = self.kept[c]
                held = (self.kmap[j, rows, :].astype(F32) * jnp.concatenate([kept, kept], 1)).astype(BF16)
                value = self.proj[rows, self.columns(j, 2)]
                full = dot_first(held, jnp.concatenate([value, jnp.ones_like(value)], 1))
                self.store_state(c, j, full)
            if step is not None:
                step(j)
            return carry

        lax.fori_loop(0, pairs, pair, 0, unroll=UNROLL)

    def map_queries(self):
        def pair(j, carry):
            self.qmap[j] = self.features(dot_mid(self.proj[:, self.columns(j, 0)], self.maps[j]))
            return carry

        lax.fori_loop(0, self.sizes.heads // 2, pair, 0, unroll=UNROLL)

    def chain_plan(self, forward):
        n = self.n
        enters = (3 * self.p) % n != 0
        leaves = (3 * (self.p + 1)) % n != 0
        if not forward:
            enters, leaves = leaves, enters
        cut = ((3 * self.p + 1) % n == 0) | ((3 * self.p + 2) % n == 0) | jnp.logical_not(enters)
        order = (0, 1, 2) if forward else (2, 1, 0)
        tok, z = self.device_of_place(jnp.clip(self.p + (1 if forward else -1), 0, n - 1))
        index = 0 if forward else 1
        message, landed, held = (
            (self.message, self.landed, self.enter)
            if forward
            else (self.message_back, self.landed_back, self.later)
        )
        half = self.sizes.state // 2
        copies = [
            self.remote(
                message.at[pl.ds(h * half, half)],
                landed.at[pl.ds(h * half, half)],
                self.chain_send.at[index, h],
                self.chain_recv.at[index, h],
                {"tok": tok, "head": z},
            )
            for h in range(2)
        ]
        return enters, leaves, cut, order, message, landed, held, copies

    def chain_sum(self, order):
        link = [self.linked(c) for c in order]
        return self.state[order[2]] + link[2] * (self.state[order[1]] + link[1] * self.state[order[0]])

    def chain_start(self, forward):
        enters, leaves, cut, order, message, landed, held, copies = self.chain_plan(forward)

        @pl.when(leaves & cut)
        def _():
            message[...] = self.chain_sum(order).astype(BF16)
            for copy in copies:
                copy.start()

        @pl.when(leaves & jnp.logical_not(cut))
        def _():
            self.chain_own[...] = self.chain_sum(order)

    def chain_pass(self, forward):
        enters, leaves, cut, order, message, landed, held, copies = self.chain_plan(forward)

        half = self.sizes.state // 2
        passed = self.linked(0) * self.linked(1) * self.linked(2)
        for h, copy in enumerate(copies):
            part = pl.ds(h * half, half)
            pl.when(enters)(copy.wait_recv)

            @pl.when(leaves & jnp.logical_not(cut))
            def _():
                message[part] = (self.chain_own[part] + passed * landed[part].astype(F32)).astype(BF16)
                copy.start()

        @pl.when(enters)
        def _():
            held[order[0]] = landed[...]

        @pl.when(jnp.logical_not(enters))
        def _():
            held[order[0]] = jnp.zeros_like(landed[...])

        for before, after in ((0, 1), (1, 2)):
            held[order[after]] = (
                self.state[order[before]] + self.linked(order[before]) * held[order[before]].astype(F32)
            ).astype(BF16)

    def chain_end(self, forward):
        enters, leaves, cut, order, message, landed, held, copies = self.chain_plan(forward)
        for copy in copies:
            pl.when(leaves)(copy.wait_send)

    def attend_inner(self, step=None):
        pairs = self.sizes.heads // 2
        left = lanes((CHUNK, 128)) < 64
        ones = jnp.where(left, 1.0, 0.0).astype(BF16)
        others = jnp.where(left, 0.0, 1.0).astype(BF16)

        def pair(j, carry):
            for c in range(3):
                rows = slice(c * CHUNK, (c + 1) * CHUNK)
                query = self.qmap[j, rows, :]
                key = self.kmap[j, rows, :]
                value = self.proj[rows, self.columns(j, 2)]
                both = jnp.concatenate([ones, ones], 1), jnp.concatenate([others, others], 1)
                raw = dot_last(jnp.concatenate([query * both[0], query * both[1]], 0), key)
                mask = self.causal[c]
                scores = jnp.concatenate([raw[0:CHUNK] * mask, raw[CHUNK:] * mask], 1).astype(BF16)
                self.scores[j, rows, :] = scores
                spread = jnp.concatenate(
                    [
                        jnp.concatenate([value * ones, ones], 1),
                        jnp.concatenate([value * others, others], 1),
                    ],
                    0,
                )
                total = dot_mid(scores, spread)
                self.acc[rows, self.columns(j, 0)] = total[:, 0:128]
                self.denom[rows, self.columns(j, 0)] = total[:, 128:256]
            if step is not None:
                step(j)
            return carry

        lax.fori_loop(0, pairs, pair, 0, unroll=UNROLL)

    def attend_outer(self):
        def pair(j, carry):
            for c in range(3):
                rows = slice(c * CHUNK, (c + 1) * CHUNK)
                usable = self.usable[c]
                outer = dot_mid(self.qmap[j, rows, :], self.expand(self.enter, c, j))
                denom = self.denom[rows, self.columns(j, 0)] + usable * outer[:, 128:256]
                numer = self.acc[rows, self.columns(j, 0)] + usable * outer[:, 0:128]
                self.denom[rows, self.columns(j, 0)] = denom
                self.mixed[rows, self.columns(j, 0)] = (numer / denom).astype(BF16)
            return carry

        lax.fori_loop(0, self.sizes.heads // 2, pair, 0, unroll=UNROLL)

    def tiles(self, out, left, weight, act):
        width = 256

        def tile(j, carry):
            cols = pl.ds(pl.multiple_of(j * width, width), width)
            out[:, cols] = act(left, weight, cols)
            return carry

        lax.fori_loop(0, out.shape[1] // width, tile, 0, unroll=True)

    def attention_out(self):
        self.tiles(self.acc, self.mixed, self.wo, lambda l, w, cols: dot_mid(l[...], w[:, cols]))
        for c in range(3):
            rows = slice(c * CHUNK, (c + 1) * CHUNK)
            hidden = self.x_rows(c) + (self.acc[rows, :] + self.branch[0:1, :])
            self.hidden[rows, :] = hidden
            self.norm_forward(hidden, 1, self.middle_t, c)

    def feed_up(self):
        root = 0.7978845608028654

        def tile(j, carry):
            cols = pl.ds(pl.multiple_of(j * TILE, TILE), TILE)
            x = dot_mid(self.normed[...], self.fc[:, cols]) + self.bias_up[0:1, cols]
            square = x * x
            half = 0.5 * jnp.tanh(x * (root + (0.044715 * root) * square)) + 0.5
            self.after[:, cols] = (x * half).astype(BF16)
            inner = x * (2.0 * root + (6.0 * 0.044715 * root) * square)
            self.before[:, cols] = (half + (half - half * half) * inner).astype(BF16)
            return carry

        lax.fori_loop(0, self.sizes.ff // TILE, tile, 0)

    def feed_down(self):
        self.tiles(self.acc, self.after, self.pt, lambda l, w, cols: dot_last(l[...], w[cols, :]))
        for c in range(3):
            rows = slice(c * CHUNK, (c + 1) * CHUNK)
            out = self.hidden[rows, :] + (self.acc[rows, :] + self.branch[1:2, :])
            self.cross[0, c] = out.astype(BF16)
            pl.when(self.section == 0)(lambda: self.cross_copy(c).start())

    def cross_copy(self, c):
        return self.remote(
            self.cross.at[self.section, c],
            self.land.at[1, c],
            self.cross_send.at[c],
            self.cross_recv.at[c],
            {"section": 1 - self.section},
        )

    def g_rows(self, c):
        return self.land[1 - self.section, c]

    def take_grad(self):
        for c in range(3):
            rows = slice(c * CHUNK, (c + 1) * CHUNK)
            self.normed[rows, :] = self.g_rows(c)
            self.grad_t[:, rows] = self.g_rows(c).T

    def feed_back(self):
        def tile(j, carry):
            cols = pl.ds(pl.multiple_of(j * TILE, TILE), TILE)
            grad = dot_mid(self.normed[...], self.pt[:, cols])
            self.before[:, cols] = (grad * self.before[:, cols].astype(F32)).astype(BF16)
            return carry

        lax.fori_loop(0, self.sizes.ff // TILE, tile, 0)
        self.tiles(self.acc, self.before, self.fc, lambda l, w, cols: dot_last(l[...], w[cols, :]))
        sums = [0.0, 0.0, 0.0, 0.0]
        for c in range(3):
            rows = slice(c * CHUNK, (c + 1) * CHUNK)
            grad = self.acc[rows, :]
            g = self.g_rows(c).astype(F32)
            unit, scale = norm_parts(self.hidden[rows, :])
            through = g + norm_back(grad, self.gains[1:2, :], unit, scale)
            self.grad_hidden[rows, :] = through
            low = through.astype(BF16)
            self.normed[rows, :] = low
            for a in range(NA):
                width = self.sizes.shard
                self.low_parts[a, rows, :] = low[:, a * width : (a + 1) * width]
            for i, value in enumerate((grad * unit, grad, through, g)):
                sums[i] = sums[i] + column_sum(value)
        self.vec[1:2, :] = sums[0]
        self.vec[3:4, :] = sums[1]
        self.vec[4:5, :] = sums[2]
        self.vec[5:6, :] = sums[3]
        dmodel = self.sizes.dmodel
        for part in range(self.sizes.ff // dmodel):
            self.vec[9 + part : 10 + part, :] = column_sum(
                self.before[:, part * dmodel : (part + 1) * dmodel].astype(F32)
            )

    def mixed_back(self):
        self.tiles(self.acc, self.normed, self.wo, lambda l, w, cols: dot_last(l[...], w[cols, :]))

    def inner_grad(self, j):
        cols = self.columns(j, 0)
        inverse = 1.0 / self.denom[:, cols]
        grad = self.acc[:, cols] * inverse
        return grad, -self.head_sum(grad * self.mixed[:, cols].astype(F32))

    def state_back(self):
        for c in range(3):
            self.state[c, self.sizes.state - 128 :, :] = jnp.zeros((128, 128), F32)

        def pair(j, carry):
            numers, denoms = self.inner_grad(j)
            for c in range(3):
                rows = slice(c * CHUNK, (c + 1) * CHUNK)
                usable = self.usable[c]
                outer = jnp.concatenate([numers[rows] * usable, denoms[rows] * usable], 1).astype(BF16)
                self.store_state(c, j, dot_first(self.qmap[j, rows, :], outer))
            return carry

        lax.fori_loop(0, self.sizes.heads // 2, pair, 0, unroll=UNROLL)

    def softmax_back(self, kind, grad):
        count = kind.shape[0]
        grad = jnp.concatenate([grad[:, 0:128], grad[:, 128:256]], 0)
        kind = jnp.concatenate([kind[:, 0:128], kind[:, 128:256]], 0).astype(F32)
        part = kind * (grad - self.head_sum(kind * grad))
        return (part[0:count] - part[count:]).astype(BF16)

    def attend_back(self, step=None):
        pairs = self.sizes.heads // 2
        place = lanes((CHUNK, 128))
        left = place < 64
        ones = jnp.where(left, 1.0, 0.0).astype(BF16)
        others = jnp.where(left, 0.0, 1.0).astype(BF16)
        single = jnp.where(place == 0, 1.0, 0.0).astype(BF16)
        double = jnp.where(place == 64, 1.0, 0.0).astype(BF16)
        corner = jnp.where(place % 64 == 0, 1.0, 0.0).astype(BF16)

        def pair(j, carry):
            cols = self.columns(j, 0)
            numers, denoms = self.inner_grad(j)
            numers, denoms = numers.astype(BF16), denoms.astype(BF16)
            grads_query = []
            for c in range(3):
                rows = slice(c * CHUNK, (c + 1) * CHUNK)
                numer, denom = numers[rows], denoms[rows]
                value = self.proj[rows, self.columns(j, 2)]
                query = self.qmap[j, rows, :]
                key = self.kmap[j, rows, :]
                mask = self.causal[c]
                usable = self.usable[c]
                both = jnp.concatenate([ones, ones], 1), jnp.concatenate([others, others], 1)
                inner = jnp.concatenate(
                    [
                        jnp.concatenate([numer * ones, denom * single], 1),
                        jnp.concatenate([numer * others, denom * double], 1),
                    ],
                    0,
                )
                grads = dot_last(inner, jnp.concatenate([value, jnp.ones_like(value)], 1))
                early = (grads[0:CHUNK] * mask).astype(BF16)
                late = (grads[CHUNK:] * mask).astype(BF16)
                grad_query = dot_mid(
                    jnp.concatenate([early, late], 1),
                    jnp.concatenate([key * both[0], key * both[1]], 0),
                )
                state = self.expand(self.enter, c, j)
                grads_query.append(
                    grad_query
                    + jnp.concatenate([usable, usable], 1)
                    * dot_last(jnp.concatenate([numer, denom * corner], 1), state)
                )
                grad_key = dot_first(
                    jnp.concatenate([early, late], 0),
                    jnp.concatenate([query * both[0], query * both[1]], 0),
                )
                scores = self.scores[j, rows, :]
                grad_value = dot_first(
                    jnp.concatenate([scores[:, 0:CHUNK], scores[:, CHUNK:]], 0),
                    jnp.concatenate([numer * ones, numer * others], 0),
                )
                self.acc[rows, cols] = grad_value
                self.denom[rows, cols] = grad_key[:, 0:128]
                self.hidden[rows, cols] = grad_key[:, 128:256]
            logits = self.softmax_back(self.qmap[j], jnp.concatenate(grads_query, 0))
            self.grad_maps[j] = dot_first(self.proj[:, cols], logits)
            self.proj[:, cols] = dot_last(logits, self.maps[j]).astype(BF16)
            if step is not None:
                step(j)
            return carry

        lax.fori_loop(0, pairs, pair, 0, unroll=UNROLL)

    def attend_back_keys(self):
        pairs = self.sizes.heads // 2
        corner = jnp.where(lanes((CHUNK, 128)) % 64 == 0, 1.0, 0.0).astype(BF16)

        def pair(j, carry):
            cols = self.columns(j, 0)
            grads_key = []
            for c in range(3):
                rows = slice(c * CHUNK, (c + 1) * CHUNK)
                kept = self.kept[c]
                value = self.proj[rows, self.columns(j, 2)]
                later = self.expand(self.later, c, j)
                grad_key = jnp.concatenate([self.denom[rows, cols], self.hidden[rows, cols]], 1)
                grads_key.append(
                    grad_key
                    + jnp.concatenate([kept, kept], 1)
                    * dot_last(jnp.concatenate([value, corner], 1), later)
                )
                grad_value = self.acc[rows, cols] + kept * dot_mid(self.kmap[j, rows, :], later[:, 0:128])
                self.proj[rows, self.columns(j, 2)] = grad_value.astype(BF16)
            logits = self.softmax_back(self.kmap[j], jnp.concatenate(grads_key, 0))
            self.grad_maps[pairs + j] = dot_first(self.proj[:, self.columns(j, 1)], logits)
            self.proj[:, self.columns(j, 1)] = dot_last(logits, self.maps[pairs + j]).astype(BF16)
            return carry

        lax.fori_loop(0, pairs, pair, 0, unroll=UNROLL)

    def project_back(self):
        self.tiles(self.acc, self.proj, self.wq, lambda l, w, cols: dot_last(l[...], w[cols, :]))
        sums = [0.0, 0.0]
        for c in range(3):
            rows = slice(c * CHUNK, (c + 1) * CHUNK)
            grad = self.acc[rows, :]
            unit, scale = norm_parts(self.x_rows(c))
            total = self.grad_hidden[rows, :] + norm_back(grad, self.gains[0:1, :], unit, scale)
            self.cross[1, c] = total.astype(BF16)
            pl.when(self.section == 1)(lambda: self.cross_copy(c).start())
            sums[0] = sums[0] + column_sum(grad * unit)
            sums[1] = sums[1] + column_sum(grad)
        self.vec[0:1, :] = sums[0]
        self.vec[2:3, :] = sums[1]
        dmodel = self.sizes.dmodel
        for part in range(3):
            self.vec[6 + part : 7 + part, :] = column_sum(
                self.proj[:, part * dmodel : (part + 1) * dmodel].astype(F32)
            )

    def partial(self, kind, a, z):
        s = self.sizes
        rows = pl.ds(pl.multiple_of(a * s.shard, 16), s.shard)
        cols = slice(z * s.ff_part, (z + 1) * s.ff_part)
        if kind == 2:
            return dot_mid(self.grad_t[rows, :], self.after[:, cols])
        if kind == 1:
            return dot_mid(self.middle_t[rows, :], self.before[:, cols])
        heads = s.heads // s.head
        width = heads * s.size
        pairs = s.heads // 2
        left = self.normed_t[rows, :]
        pieces = [
            dot_mid(left, self.proj[:, part * s.dmodel + z * width : part * s.dmodel + (z + 1) * width])
            for part in range(3)
        ]
        pieces.append(dot_first(self.mixed[:, z * width : (z + 1) * width], self.low_parts[a]))
        top = jnp.concatenate(pieces, 1)
        half = lanes((16, 128)) < 64
        blocks = []
        for k in range(2 * heads):
            head = heads * z + k // 2
            first = pl.multiple_of(64 * (head % 2) + 32 * (a % 2) + 16 * (k % 2), 16)
            block = self.grad_maps[(a // 2) * pairs + head // 2, pl.ds(first, 16), :]
            keep = half if head % 2 == 0 else jnp.logical_not(half)
            block = jnp.where(keep, block, 0.0)
            blocks.append(block + pltpu.roll(block, 64, 1))
        return jnp.concatenate([top, jnp.concatenate(blocks, 1)], 0)

    def first_slot(self, kind, index):
        if kind == 0:
            return self.pair_a.at[index]
        return self.slab.at[8 * (kind - 1) + index, pl.ds(0, self.sizes.shard)]

    def slot_rows(self, ref, index, kind):
        rows = self.sizes.shard + (16 if kind == 0 else 0)
        return ref.at[kind, index, pl.ds(0, rows)]

    def pair_copy(self, kind, index):
        rows = self.sizes.shard + (16 if kind == 0 else 0)
        return self.remote(
            self.stage.at[index, pl.ds(0, rows)],
            self.first_slot(kind, index),
            self.pair_send.at[kind, index],
            self.pair_recv.at[kind, index],
            self.towards(3),
        )

    def reduce_pair(self, kind):
        nz = self.sizes.head
        rows = self.sizes.shard + (16 if kind == 0 else 0)
        for near in range(2):
            y = self.y if near else 1 - self.y
            for z in self.outward:
                index = near * nz + z
                if kind != self.kinds[0]:
                    self.pair_copy(self.kinds[self.kinds.index(kind) - 1], index).wait_send()
                self.stage[index, 0:rows, :] = self.partial(kind, 2 * y + 1 - self.c, z).astype(BF16)
                self.pair_copy(kind, index).start()

    def across_copy(self, kind, z):
        return self.remote(
            self.first_slot(kind, z),
            self.slot_rows(self.across, z, kind),
            self.across_send.at[kind, z],
            self.across_recv.at[kind, z],
            self.towards(2),
        )

    def reduce_across(self, kind):
        for z in self.outward:
            self.pair_copy(kind, z).wait_recv()
            slot = self.first_slot(kind, z)
            total = self.partial(kind, 2 * (1 - self.y) + self.c, z) + slot[...].astype(F32)
            slot[...] = total.astype(BF16)
            self.across_copy(kind, z).start()

    def reduce_here(self, kind, places):
        nz = self.sizes.head
        for z in places:
            self.pair_copy(kind, nz + z).wait_recv()
            total = self.partial(kind, 2 * self.y + self.c, z) + self.first_slot(kind, nz + z)[...].astype(F32)
            self.across_copy(kind, z).wait_recv()
            slot = self.slot_rows(self.across, z, kind)
            slot[...] = (total + slot[...].astype(F32)).astype(BF16)
            pl.when(self.z != z)(lambda: self.line_copy(kind, z).start())

    def line_copy(self, kind, z):
        nz = self.sizes.head
        index = (self.z - z + nz) % nz - 1
        return self.remote(
            self.slot_rows(self.across, z, kind),
            self.slot_rows(self.line, jnp.maximum(index, 0), kind),
            self.line_send.at[kind, z],
            self.line_recv.at[kind, jnp.maximum(index, 0)],
            self.cell(self.a, z),
        )

    def reduce_last(self, kind):
        nz = self.sizes.head
        source, out = self.reduced(kind)
        total = self.slot_rows(self.across, self.z, kind)[...].astype(F32)
        for index in range(nz - 1):
            slot = self.slot_rows(self.line, index, kind)
            self.remote(
                slot, slot, self.line_send.at[kind, 0], self.line_recv.at[kind, index], self.cell(self.a, self.z)
            ).wait_recv()
            total = total + slot[...].astype(F32)
        source[...] = total
        pltpu.make_async_copy(source, out, self.reduced_send.at[kind]).start()

    def reduced(self, kind):
        shard = self.sizes.shard
        if kind == 0:
            return self.denom.at[pl.ds(0, shard + 16)], self.grad_a
        if kind == 1:
            return self.acc.at[pl.ds(0, shard)], self.grad_f
        return self.acc.at[pl.ds(shard, shard)], self.grad_p

    def reduce_end(self):
        nz = self.sizes.head
        for kind in self.kinds:
            source, out = self.reduced(kind)
            pltpu.make_async_copy(source, out, self.reduced_send.at[kind]).wait()
        for z in range(2 * nz):
            self.pair_copy(self.kinds[-1], z).wait_send()
        for kind in self.kinds:
            for z in range(nz):
                self.across_copy(kind, z).wait_send()
            for z in range(nz):
                pl.when(self.z != z)(lambda: self.line_copy(kind, z).wait_send())

    def vector_copy(self, stage):
        nz = self.sizes.head
        device = (
            self.towards(3),
            self.towards(2),
            self.cell(self.a, self.z + 1 - 2 * (self.z % 2)),
            self.cell(self.a, (self.z + nz // 2) % nz),
        )[stage]
        return self.remote(
            self.vec_out.at[stage],
            self.vec_in.at[stage],
            self.vec_send.at[stage],
            self.vec_recv.at[stage],
            device,
        )

    def vector_start(self, stage):
        self.vec_out[stage] = self.vec[...]
        self.vector_copy(stage).start()

    def vector_end(self, stage):
        self.vector_copy(stage).wait_recv()
        self.vec[...] = self.vec[...] + self.vec_in[stage]

    def run(self):
        nz = self.sizes.head
        self.kinds = (2, 1, 0)
        self.outward = [z for pair in zip(range(nz // 2), range(nz - 1, nz // 2 - 1, -1)) for z in pair]
        self.place()
        first = self.section == 0
        second = self.section == 1
        self.take_params()
        self.barrier()
        self.weight_own(0)
        self.deal()
        place = lax.broadcasted_iota(jnp.int32, (256, 128), 0) % 128 // 64
        self.ones[...] = jnp.where(place == lanes((256, 128)) // 64, 1.0, 0.0).astype(BF16)
        self.vec[...] = jnp.zeros_like(self.vec)
        start, steps, others, late = self.weight_steps()
        for step in start:
            step()

        @pl.when(second)
        def _():
            for step in others:
                step()
            for d in range(nz):
                self.relay(d, True)

        at = [0]

        def some_weights(number):
            taken = steps[at[0] : at[0] + number]
            at[0] += number

            @pl.when(first)
            def _():
                for step in taken:
                    step()

        self.assemble()
        self.dealt()
        self.masks()
        some_weights(2)
        for c in range(3):
            pl.when(second)(lambda: self.cross_copy(c).wait_recv())
        self.project()
        some_weights(1)

        def between(j):
            for k in range(3):

                @pl.when(first & (j == 2 * k + 1))
                def _():
                    steps[at[0] + k]()

        self.map_keys(between)
        at[0] += 3
        self.chain_start(True)
        self.map_queries()
        n = self.n
        count = self.sizes.heads // 2
        depth = self.p - ((3 * self.p) // n * n) // 3
        when = jnp.clip(5 * (depth - 1) // 2, 0, count - 1)

        def meanwhile(j):
            for k in range(count):
                pl.when(first & (j == k))(steps[at[0] + k])
            pl.when(j == when)(lambda: self.chain_pass(True))

        self.attend_inner(meanwhile)
        at[0] += count
        pl.when(second)(late[0])
        self.attend_outer()
        some_weights(1)
        pl.when(second)(late[1])
        self.attention_out()
        some_weights(2)
        pl.when(second)(late[2])
        self.feed_up()
        some_weights(len(steps))

        @pl.when(second)
        def _():
            for step in late[3:]:
                step()

        self.weight_end(0)
        pl.semaphore_signal(self.free, inc=1, device_id=self.towards(3), device_id_type=MESH)
        self.feed_down()

        @pl.when(first)
        def _():
            self.send_home(0)
            for c in range(3):
                self.cross_copy(c).wait_recv()

        self.take_grad()

        @pl.when(first)
        def _():
            pl.semaphore_wait(self.free, 1)
            self.reduce_pair(2)
            self.reduce_across(2)

        self.feed_back()

        hold = self.p % (2 * nz) < 2
        pl.when(first)(lambda: self.reduce_pair(1))
        self.mixed_back()
        self.state_back()
        self.chain_start(False)
        pl.when(first & jnp.logical_not(hold))(lambda: self.reduce_across(1))
        n = self.n
        depth = (((3 * self.p + 2) // n + 1) * n - 1) // 3 - self.p
        when = jnp.minimum(jnp.maximum(2 * depth - 2, 0), self.sizes.heads // 2 - 1)

        def during(j):
            pl.when(j == when)(lambda: self.chain_pass(False))

        self.attend_back(during)

        pl.when(first & hold)(lambda: self.reduce_across(1))
        pl.when(first)(lambda: self.reduce_here(2, self.outward))
        self.attend_back_keys()
        self.project_back()

        self.vector_start(0)

        @pl.when(second)
        def _():
            pl.semaphore_wait(self.free, 1)
            self.reduce_pair(2)
            self.reduce_across(2)
            self.reduce_pair(1)
            self.reduce_across(1)

        self.reduce_pair(0)
        self.vector_end(0)
        self.vector_start(1)
        self.reduce_across(0)
        pl.when(second)(lambda: self.send_home(0))
        pl.when(second)(lambda: self.reduce_here(2, self.outward))
        self.reduce_here(1, self.outward)
        self.vector_end(1)
        self.vector_start(2)
        self.reduce_last(2)
        self.reduce_here(0, self.outward)
        self.send_home(1)
        self.vector_end(2)
        self.vector_start(3)
        self.reduce_last(1)
        self.reduce_last(0)
        self.vector_end(3)
        for stage in range(4):
            self.vector_copy(stage).wait_send()
        self.grad_gains[...] = self.vec[0:2, :]
        self.grad_biases[...] = self.vec[2:4, :]
        self.grad_branch[...] = self.vec[4:6, :]
        self.grad_bias_in[...] = self.vec[6:9, :]
        dmodel = self.sizes.dmodel
        for part in range(self.sizes.ff // dmodel):
            self.grad_bias_up[:, part * dmodel : (part + 1) * dmodel] = self.vec[9 + part : 10 + part, :]
        self.deal_end()
        self.weight_end(1)
        self.weight_end(2)
        for c in range(3):
            self.cross_copy(c).wait_send()
        self.chain_end(True)
        self.chain_end(False)
        self.reduce_end()
        self.home_end(0)
        self.home_end(1)


def scratch(s):
    rows, dmodel, ff, shard = 3 * CHUNK, s.dmodel, s.ff, s.shard
    pairs, nz, state = s.heads // 2, s.head, s.state
    vmem, dma = pltpu.VMEM, pltpu.SemaphoreType.DMA
    cells = NA * nz
    return dict(
        seg_in=vmem((3, 8, CHUNK), F32),
        gains=vmem((2, dmodel), F32),
        biases=vmem((2, dmodel), F32),
        branch=vmem((2, dmodel), F32),
        bias_in=vmem((3, dmodel), F32),
        bias_up=vmem((1, ff), F32),
        vec=vmem((16, dmodel), F32),
        land=vmem((2, 3, CHUNK, dmodel), BF16),
        segs=vmem((3, 8, CHUNK), F32),
        slab=vmem((cells, shard + 16, dmodel), BF16),
        fc=vmem((dmodel, ff), BF16),
        pt=vmem((dmodel, ff), BF16),
        wq=vmem((dmodel, 3 * dmodel), BF16),
        wo=vmem((dmodel, dmodel), BF16),
        maps=vmem((2 * pairs, 128, 128), BF16),
        ones=vmem((256, 128), BF16),
        causal=vmem((3, CHUNK, CHUNK), F32),
        usable=vmem((3, CHUNK, CHUNK), F32),
        kept=vmem((3, CHUNK, CHUNK), F32),
        normed=vmem((rows, dmodel), BF16),
        normed_t=vmem((dmodel, rows), BF16),
        middle_t=vmem((dmodel, rows), BF16),
        grad_t=vmem((dmodel, rows), BF16),
        proj=vmem((rows, 3 * dmodel), BF16),
        qmap=vmem((pairs, rows, 256), BF16),
        kmap=vmem((pairs, rows, 256), BF16),
        scores=vmem((pairs, rows, 256), BF16),
        denom=vmem((rows, dmodel), F32),
        mixed=vmem((rows, dmodel), BF16),
        acc=vmem((rows, dmodel), F32),
        hidden=vmem((rows, dmodel), F32),
        grad_hidden=vmem((rows, dmodel), F32),
        after=vmem((rows, ff), BF16),
        before=vmem((rows, ff), BF16),
        low_parts=vmem((NA, rows, shard), BF16),
        cross=vmem((2, 3, CHUNK, dmodel), BF16),
        state=vmem((3, state, 128), F32),
        chain_own=vmem((state, 128), F32),
        enter=vmem((3, state, 128), BF16),
        later=vmem((3, state, 128), BF16),
        message=vmem((state, 128), BF16),
        landed=vmem((state, 128), BF16),
        message_back=vmem((state, 128), BF16),
        landed_back=vmem((state, 128), BF16),
        grad_maps=vmem((2 * pairs, 128, 128), F32),
        stage=vmem((2 * nz, shard + 16, dmodel), BF16),
        pair_a=vmem((2 * nz, shard + 16, dmodel), BF16),
        across=vmem((3, nz, shard + 16, dmodel), BF16),
        line=vmem((3, nz - 1, shard + 16, dmodel), BF16),
        vec_out=vmem((4, 16, dmodel), F32),
        vec_in=vmem((4, 16, dmodel), F32),
        deal_send=dma((3,)),
        deal_recv=dma((3,)),
        segs_send=dma((3,)),
        segs_recv=dma((3,)),
        ag_send=dma((3, 4, cells)),
        ag_recv=dma((3, cells)),
        ag_own=dma((3,)),
        relay_send=dma((nz,)),
        relay_recv=dma((nz,)),
        cross_send=dma((3,)),
        cross_recv=dma((3,)),
        chain_send=dma((2, 2)),
        chain_recv=dma((2, 2)),
        home_send=dma((2, 3)),
        home_recv=dma((2, 3)),
        pair_send=dma((3, 2 * nz)),
        pair_recv=dma((3, 2 * nz)),
        across_send=dma((3, nz)),
        across_recv=dma((3, nz)),
        line_send=dma((3, nz)),
        line_recv=dma((3, nz - 1)),
        reduced_send=dma((3,)),
        vec_send=dma((4,)),
        vec_recv=dma((4,)),
        free=pltpu.SemaphoreType.REGULAR,
    )


def train_step(s, *args):
    held = scratch(s)
    anywhere = pl.BlockSpec(memory_space=pl.ANY)
    inside = pl.BlockSpec(memory_space=pltpu.VMEM)
    dmodel, shard = s.dmodel, s.shard
    given = dict(
        x_in=anywhere,
        g_in=anywhere,
        seg_ids=inside,
        sh_a=anywhere,
        sh_f=anywhere,
        sh_p=anywhere,
        gains_in=inside,
        biases_in=inside,
        branch_in=inside,
        bias_in_in=inside,
        bias_up_in=inside,
    )
    made = dict(
        out_rows=anywhere,
        grad_rows=anywhere,
        grad_a=anywhere,
        grad_f=anywhere,
        grad_p=anywhere,
        grad_gains=inside,
        grad_biases=inside,
        grad_branch=inside,
        grad_bias_in=inside,
        grad_bias_up=inside,
    )
    names = list(given) + list(made) + list(held)

    def body(*refs):
        Step(s, names, refs).run()

    return pl.pallas_call(
        body,
        out_shape=(
            jax.ShapeDtypeStruct((3, CHUNK, dmodel), BF16),
            jax.ShapeDtypeStruct((3, CHUNK, dmodel), BF16),
            jax.ShapeDtypeStruct((shard + 16, dmodel), F32),
            jax.ShapeDtypeStruct((shard, dmodel), F32),
            jax.ShapeDtypeStruct((shard, dmodel), F32),
            jax.ShapeDtypeStruct((2, dmodel), F32),
            jax.ShapeDtypeStruct((2, dmodel), F32),
            jax.ShapeDtypeStruct((2, dmodel), F32),
            jax.ShapeDtypeStruct((3, dmodel), F32),
            jax.ShapeDtypeStruct((1, s.ff), F32),
        ),
        in_specs=list(given.values()),
        out_specs=tuple(made.values()),
        scratch_shapes=list(held.values()),
        compiler_params=pltpu.CompilerParams(
            collective_id=0, has_side_effects=True, vmem_limit_bytes=64 * 1024 * 1024
        ),
        name="train_step",
    )(*args)


def local(
    block_input,
    segment_ids,
    output_grad,
    norm_gains,
    norm_biases,
    qkv_weight,
    qkv_bias,
    feature_maps,
    out_weight,
    branch_bias,
    fc_weight,
    fc_bias,
    proj_weight,
):
    nt, nz = lax.axis_size("tok"), lax.axis_size("head")
    micro, rows, dmodel = block_input.shape
    heads = feature_maps.shape[1] * nz
    ff = fc_bias.shape[1]
    size = dmodel // heads
    group = nt // NA
    sizes = Sizes(
        tok=nt,
        head=nz,
        micro=micro,
        dmodel=dmodel,
        heads=heads,
        size=size,
        ff=ff,
        ff_part=ff // nz,
        shard=dmodel // NA,
        state=heads // 2 * 128 + 128,
    )
    assert micro == 3 and rows == CHUNK and size == 64 and nt % NA == 0
    groups = [[group * a + b for b in range(group)] for a in range(NA)]

    def widen(part, dim):
        if group == 1:
            return part
        return lax.all_gather(part, "tok", axis=dim, tiled=True, axis_index_groups=groups)

    def narrow(part, dim):
        if group == 1:
            return part
        return lax.psum_scatter(part, "tok", scatter_dimension=dim, tiled=True, axis_index_groups=groups)

    shard = dmodel // NA
    width = dmodel // nz
    w_in = widen(qkv_weight[0], 0).reshape(shard, 3 * width)
    w_out = widen(out_weight[0], 1)
    maps = widen(feature_maps[0], 1)
    w_up = widen(fc_weight[0], 0)
    w_down = widen(proj_weight[0], 1).T
    maps = maps.reshape(2 * heads // nz, 16, size)
    maps = jnp.concatenate([maps, maps], 2).transpose(1, 0, 2).reshape(16, 4 * heads // nz * size)
    sh_a = jnp.concatenate([jnp.concatenate([w_in, w_out], 1), maps], 0)
    out_rows, grad_rows, grad_a, grad_f, grad_p, *vectors = train_step(
        sizes,
        block_input,
        output_grad,
        segment_ids,
        sh_a,
        w_up,
        w_down,
        norm_gains[0],
        norm_biases[0],
        branch_bias[0],
        qkv_bias[0],
        fc_bias,
    )
    if group > 1:
        vectors = [jnp.sum(lax.all_gather(v, "tok", axis=0, axis_index_groups=groups), 0) for v in vectors]
    grad_in = narrow(grad_a[:shard, : 3 * width].reshape(shard, 3, width), 0)
    grad_out = narrow(grad_a[:shard, 3 * width :], 1)
    grad_maps = grad_a[shard:].reshape(16, 2 * heads // nz, 2 * size)[:, :, :size]
    grad_maps = narrow(grad_maps.transpose(1, 0, 2).reshape(heads // nz, 2 * 16 * size), 1)
    return (
        out_rows[None].astype(F32),
        grad_rows[None].astype(F32),
        vectors[0][None],
        vectors[1][None],
        grad_in[None],
        vectors[3][None],
        grad_maps[None],
        grad_out[None],
        vectors[2][None],
        narrow(grad_f, 0)[None],
        vectors[4],
        narrow(grad_p, 0).T[None],
    )


def solution(mesh):
    in_specs = (
        P(None, ("tok", "head"), None),
        P(None, "tok"),
        P(None, ("tok", "head"), None),
        P("section", None, None),
        P("section", None, None),
        P("section", "tok", None, "head"),
        P("section", None, None),
        P("section", "head", "tok"),
        P("section", "head", "tok"),
        P("section", None, None),
        P("section", "tok", "head"),
        P("section", None),
        P("section", "head", "tok"),
    )
    out_specs = (
        P("section", None, ("tok", "head"), None),
        P("section", None, ("tok", "head"), None),
        P("section", None, None),
        P("section", None, None),
        P("section", "tok", None, "head"),
        P("section", None, None),
        P("section", "head", "tok"),
        P("section", "head", "tok"),
        P("section", None, None),
        P("section", "tok", "head"),
        P("section", None),
        P("section", "head", "tok"),
    )
    return jax.shard_map(local, mesh=mesh, in_specs=in_specs, out_specs=out_specs, check_vma=False)
```
